32 devices in a mesh: gx: 8 (over z, x), gy: 4 (over y, core).
Axes of the slice: x: 2, y: 2, z: 4, core: 2. Of those that a mesh axis runs over, the one named last changes fastest.
Arguments:
- moving_image: bfloat16 [16, 256, 1024], P(None, 'gx', 'gy'), may hold values from -6 to 6, as said below
- fixed_image: bfloat16 [16, 256, 1024], P(None, 'gx', 'gy'), may hold values from -6 to 6, as said below
- velocity: float32 [3, 16, 256, 1024], P(None, None, 'gx', 'gy'), may hold values from 0 to 1
- offsets: int32 [3, 16, 8], P(None, 'gx', 'gy'), may hold values from -7 to 7, as said below
- tissue: int32 [16, 8], P('gx', 'gy'), may hold values from 0 to 1, as said below
Outputs:
- update: float32 [3, 16, 256, 1024], P(None, None, 'gx', 'gy')
- similarity_loss: float32 [], replicated
The draws below stay inside these ranges and needn't reach their ends.
Inputs may be any that keep to these rules, and one draw needn't show every extreme that they name: `moving_image`: the images stay within -6 to 6. `fixed_image`: the images stay within -6 to 6. `offsets`: channel 0 lies in -2 to 2, channels 1 and 2 in -7 to 7; each end is taken by some block. 1 marks a block that holds tissue; some blocks hold tissue.
All inputs are finite; a program needn't handle non-finite values.
Results may differ from the reference program's by a relative error of at most 0.0011.
Values may be sent and summed in bfloat16 or wider, within the bound.
A program may use at most 64 MiB of HBM per device.

```python
import math
import jax
import jax.numpy as jnp
from jax import lax

DEPTH = 16
BX = 16
BY = 128
REACH = 7
ZREACH = 2
NX = 256
NY = 1024


def base_pattern(key):
    pattern_key = jax.random.fold_in(key, 101)
    subkeys = jax.random.split(pattern_key, 5)
    wave_x = jax.random.randint(subkeys[0], (6,), -4, 5)
    wave_y = jax.random.randint(subkeys[1], (6,), -4, 5)
    wave_z = jax.random.randint(subkeys[2], (6,), -2, 3)
    phases = jax.random.uniform(subkeys[3], (6,), minval=0.0, maxval=2.0 * math.pi)
    amplitude = jax.random.uniform(subkeys[4], (6,), minval=0.3, maxval=0.6)
    index_z = jnp.arange(DEPTH, dtype=jnp.int32)[:, None, None]
    index_x = jnp.arange(NX, dtype=jnp.int32)[None, :, None]
    index_y = jnp.arange(NY, dtype=jnp.int32)[None, None, :]
    pattern = jnp.zeros((DEPTH, NX, NY), jnp.float32)
    for wave in range(6):
        cycle = (wave_x[wave] * index_x + wave_y[wave] * index_y) % 256
        vertical = wave_z[wave] * index_z % 32
        angle = 2.0 * math.pi / 256.0 * cycle.astype(jnp.float32) + 2.0 * math.pi / 32.0 * vertical.astype(jnp.float32) + phases[wave]
        pattern = pattern + amplitude[wave] * jnp.sin(angle)
    return pattern


def image_noise(key, salt):
    noise_key = jax.random.fold_in(key, salt)
    return 0.6 * jnp.clip(jax.random.normal(noise_key, (DEPTH, NX, NY), jnp.float32), -4.0, 4.0)


def draw_moving_image(key, part):
    return (base_pattern(key) + image_noise(key, 303)).astype(jnp.bfloat16)


def draw_fixed_image(key, part):
    return (base_pattern(key) + image_noise(key, 202)).astype(jnp.bfloat16)


def draw_offsets(key, part):
    block_rows = NX // BX
    block_cols = NY // BY
    subkeys = jax.random.split(jax.random.fold_in(key, 404), 4)
    vertical = jax.random.randint(subkeys[0], (1, block_rows, block_cols), -ZREACH, ZREACH + 1)
    planar = jax.random.randint(subkeys[1], (2, block_rows, block_cols), -REACH, REACH + 1)
    shifts = jnp.concatenate([vertical, planar], axis=0)
    total_blocks = block_rows * block_cols
    flat_index = jnp.arange(total_blocks, dtype=jnp.int32).reshape(block_rows, block_cols)
    high_pick = jax.random.randint(subkeys[2], (), 0, total_blocks)
    low_pick = (high_pick + 1 + jax.random.randint(subkeys[3], (), 0, total_blocks - 1)) % total_blocks
    reach_bound = jnp.array([ZREACH, REACH, REACH], jnp.int32)[:, None, None]
    shifts = jnp.where((flat_index == high_pick)[None], reach_bound, shifts)
    shifts = jnp.where((flat_index == low_pick)[None], -reach_bound, shifts)
    return shifts.astype(jnp.int32)


def draw_tissue(key, part):
    block_rows = NX // BX
    block_cols = NY // BY
    draw_level = jax.random.randint(jax.random.fold_in(key, 505), (block_rows, block_cols), 0, block_rows)
    row_index = jnp.arange(block_rows, dtype=jnp.int32)[:, None]
    return (draw_level < row_index + block_rows // 4).astype(jnp.int32)


def level_of(stream_key, shape, shards, smallest, top_value):
    def one(position, blocks):
        draws = jax.random.uniform(jax.random.fold_in(jax.random.fold_in(stream_key, 6), position), (blocks,), jnp.float32, smallest / len(shards), top_value / len(shards))
        return jnp.repeat(jnp.exp(draws), shape[position] // blocks).reshape((-1,) + (1,) * (len(shape) - position - 1))

    gain = one(*shards[0])
    for cut in shards[1:]:
        gain = gain * one(*cut)
    return gain


def setup_inputs(seed: int = 0) -> dict:
    keys = jax.random.split(jax.random.key(seed), 6)
    return {
        "moving_image": draw_moving_image(jax.random.fold_in(keys[5], 71), 0),
        "fixed_image": draw_fixed_image(jax.random.fold_in(keys[5], 71), 0),
        "velocity": jnp.clip(1.0 * jax.random.uniform(keys[2], (3, DEPTH, NX, NY), jnp.float32) ** level_of(keys[2], (3, DEPTH, NX, NY), ((2, 8), (3, 4)), -0.2, 0.2), 0.0, 1.0),
        "offsets": draw_offsets(jax.random.fold_in(keys[5], 71), 0),
        "tissue": draw_tissue(jax.random.fold_in(keys[5], 71), 0),
    }


BOX_RADIUS = 4
GAUSS_RADIUS = 7
GAUSS_SIGMA = 3.0
WINDOW_COUNT = 729.0
VAR_EPSILON = 1e-5
STEP_RATE = 16.0


def gauss_weights():
    raw_weights = [math.exp(-float(tap * tap) / (2.0 * GAUSS_SIGMA * GAUSS_SIGMA)) for tap in range(-GAUSS_RADIUS, GAUSS_RADIUS + 1)]
    weight_total = sum(raw_weights)
    return [weight_value / weight_total for weight_value in raw_weights]


def box_weights():
    return [1.0] * (2 * BOX_RADIUS + 1)


def filter_valid(volume, weights, dim_index):
    length = volume.shape[dim_index] - (len(weights) - 1)
    summed = weights[0] * lax.slice_in_dim(volume, 0, length, axis=dim_index)
    for tap_index in range(1, len(weights)):
        summed = summed + weights[tap_index] * lax.slice_in_dim(volume, tap_index, tap_index + length, axis=dim_index)
    return summed


def filter_padded(volume, weights, dim_index):
    radius = (len(weights) - 1) // 2
    widths = [(0, 0)] * volume.ndim
    widths[dim_index] = (radius, radius)
    return filter_valid(jnp.pad(volume, widths), weights, dim_index)


def interpolate(sampler, fraction):
    weights_z = (1.0 - fraction[0], fraction[0])
    weights_x = (1.0 - fraction[1], fraction[1])
    weights_y = (1.0 - fraction[2], fraction[2])
    slope_signs = (-1.0, 1.0)
    results = None
    for corner_z in (0, 1):
        for corner_x in (0, 1):
            for corner_y in (0, 1):
                sample = sampler(corner_z, corner_x, corner_y)
                planar = weights_x[corner_x] * weights_y[corner_y]
                terms = (weights_z[corner_z] * planar * sample,
                         slope_signs[corner_z] * planar * sample,
                         weights_z[corner_z] * slope_signs[corner_x] * weights_y[corner_y] * sample,
                         weights_z[corner_z] * weights_x[corner_x] * slope_signs[corner_y] * sample)
                if results is None:
                    results = terms
                else:
                    results = tuple(results[item] + terms[item] for item in range(4))
    return results


def window_terms(image_sum, target_sum, image_square, target_square, product_sum, tissue_mask):
    cross_sum = product_sum - image_sum * target_sum / WINDOW_COUNT
    image_var = image_square - image_sum * image_sum / WINDOW_COUNT
    target_var = target_square - target_sum * target_sum / WINDOW_COUNT
    denominator = image_var * target_var + VAR_EPSILON
    ncc_value = cross_sum * cross_sum / denominator
    quotient = cross_sum / denominator
    second = quotient * quotient * target_var
    adjoint_sum = (2.0 / WINDOW_COUNT) * tissue_mask * (quotient * target_sum - second * image_sum)
    adjoint_square = tissue_mask * second
    adjoint_product = -2.0 * tissue_mask * quotient
    return ncc_value, adjoint_sum, adjoint_square, adjoint_product


def box_full(volume):
    weights = box_weights()
    return filter_padded(filter_padded(filter_padded(volume, weights, 0), weights, 1), weights, 2)


def reference(moving_image, fixed_image, velocity, offsets, tissue):
    slab_depth, extent_x, extent_y = moving_image.shape
    depth_pad = ZREACH + 1
    plane_pad = REACH + 1
    padded = jnp.pad(moving_image, ((depth_pad, depth_pad), (plane_pad, plane_pad), (plane_pad, plane_pad)))
    voxel_offsets = jnp.repeat(jnp.repeat(offsets, BX, axis=1), BY, axis=2).astype(jnp.int32)
    index_z = jnp.arange(slab_depth, dtype=jnp.int32)[:, None, None] + voxel_offsets[0][None] + depth_pad
    index_x = (jnp.arange(extent_x, dtype=jnp.int32)[:, None] + voxel_offsets[1] + plane_pad)[None]
    index_y = (jnp.arange(extent_y, dtype=jnp.int32)[None, :] + voxel_offsets[2] + plane_pad)[None]

    def sampler(corner_z, corner_x, corner_y):
        return padded[index_z + corner_z, index_x + corner_x, index_y + corner_y].astype(jnp.float32)

    warped, slope_z, slope_x, slope_y = interpolate(sampler, velocity)
    warped_low = warped.astype(jnp.bfloat16)
    image_value = lax.optimization_barrier(warped_low).astype(jnp.float32)
    target_value = fixed_image.astype(jnp.float32)
    tissue_mask = jnp.repeat(jnp.repeat(tissue, BX, axis=0), BY, axis=1).astype(jnp.float32)[None]
    ncc_value, adjoint_sum, adjoint_square, adjoint_product = window_terms(
        box_full(image_value), box_full(target_value), box_full(image_value * image_value),
        box_full(target_value * target_value), box_full(image_value * target_value), tissue_mask)
    grad_image = box_full(adjoint_sum) + 2.0 * image_value * box_full(adjoint_square) + target_value * box_full(adjoint_product)
    gradient = jnp.stack([grad_image * slope_z, grad_image * slope_x, grad_image * slope_y])
    gauss = gauss_weights()
    smoothed = filter_padded(filter_padded(filter_padded(gradient, gauss, 2), gauss, 3), gauss, 1)
    update = -STEP_RATE * smoothed
    tissue_total = jnp.sum(tissue).astype(jnp.float32)
    similarity_loss = -jnp.sum(tissue_mask * ncc_value) / (tissue_total * float(BX * BY * DEPTH))
    return update, similarity_loss
```

```python
import functools
import math

import jax
import jax.numpy as jnp
import numpy as np
from jax import lax
from jax.experimental import pallas as pl
from jax.experimental.pallas import tpu as pltpu
from jax.sharding import PartitionSpec as P

BX = 16
BY = 128
ZREACH = 2
BOX = 4
GAUSS_RADIUS = 7
GAUSS_SIGMA = 3.0
COUNT = 729.0
EPS = 1e-05
STEP_RATE = 16.0
HALO = 16
GHALO = 8
GROUP = 4
F32 = jnp.float32
BF16 = jnp.bfloat16
MESH = pl.DeviceIdType.MESH

DIRS = [(-1, 0), (1, 0), (0, -1), (0, 1), (-1, -1), (-1, 1), (1, -1), (1, 1)]


def dot(a, b):
    return jnp.dot(a, b, preferred_element_type=F32)


def split2(x):
    h = x.astype(BF16)
    return h, (x - h.astype(F32)).astype(BF16)


def split3(x):
    h = x.astype(BF16)
    r = x - h.astype(F32)
    m = r.astype(BF16)
    return h, m, (r - m.astype(F32)).astype(BF16)


def halo_refs(direction, rows, center, left, right):
    dx, dy = direction
    src_rows = {-1: pl.ds(HALO, HALO), 0: pl.ds(HALO, rows), 1: pl.ds(rows, HALO)}[dx]
    dst_rows = {-1: pl.ds(HALO + rows, HALO), 0: pl.ds(HALO, rows), 1: pl.ds(0, HALO)}[dx]
    cols = center.shape[2]
    if dy == 0:
        return center.at[:, src_rows, :], center.at[:, dst_rows, :]
    if dy < 0:
        return center.at[:, src_rows, pl.ds(0, BY)], right.at[:, dst_rows, :]
    return center.at[:, src_rows, pl.ds(cols - BY, BY)], left.at[:, dst_rows, :]


def fused_kernel(
    nx, ny,
    off_ref, tis_ref, mov_ref, fix_ref, vel_hbm,
    gh_ref, gl_ref, acc_ref,
    mC, mL, mR, fC, fL, fR, wC, wL, wR, sC, sL, sR,
    vel, sF, T, Y, A, by_ref, bx_ref,
    vel_sem, send_sem, recv_sem,
):
    depth, rows, cols = mov_ref.shape
    ext = rows + 2 * HALO
    wide = cols + BY
    gx, gy = lax.axis_index("gx"), lax.axis_index("gy")

    def exists(d):
        dx, dy = d
        c = None
        for cond in (
            (gx > 0) if dx < 0 else (gx < nx - 1) if dx > 0 else None,
            (gy > 0) if dy < 0 else (gy < ny - 1) if dy > 0 else None,
        ):
            if cond is not None:
                c = cond if c is None else jnp.logical_and(c, cond)
        return c

    has = [exists(d) for d in DIRS]

    vel_copy = pltpu.make_async_copy(vel_hbm, vel, vel_sem)
    vel_copy.start()

    barrier = pltpu.get_barrier_semaphore()
    for i, (dx, dy) in enumerate(DIRS):
        @pl.when(has[i])
        def _():
            pl.semaphore_signal(barrier, inc=1, device_id=(gx + dx, gy + dy), device_id_type=MESH)

    def clear(center, left, right):
        for i, (dx, dy) in enumerate(DIRS):
            _, dst = halo_refs((-dx, -dy), rows, center, left, right)

            @pl.when(jnp.logical_not(has[i]))
            def _():
                dst[...] = jnp.zeros(dst.shape, dst.dtype)

    mC[:, HALO : HALO + rows, :] = mov_ref[...]
    def line(g, n):
        return 1 + jnp.where(g > 0, 1, 0) + jnp.where(g < n - 1, 1, 0)

    pl.semaphore_wait(barrier, line(gx, nx) * line(gy, ny) - 1)

    def copies(t, center, left, right):
        out = []
        for i, (dx, dy) in enumerate(DIRS):
            src, dst = halo_refs((dx, dy), rows, center, left, right)
            out.append(
                pltpu.make_async_remote_copy(
                    src_ref=src, dst_ref=dst,
                    send_sem=send_sem.at[t, i], recv_sem=recv_sem.at[t, i],
                    device_id=(gx + dx, gy + dy), device_id_type=MESH,
                )
            )
        return out

    def start(cs):
        for i, c in enumerate(cs):
            @pl.when(has[i])
            def _():
                c.start()

    def wait_recv(cs):
        for i, c in enumerate(cs):
            j = DIRS.index((-DIRS[i][0], -DIRS[i][1]))

            @pl.when(has[j])
            def _():
                c.wait_recv()

    def wait_send(cs):
        for i, c in enumerate(cs):
            @pl.when(has[i])
            def _():
                c.wait_send()

    m_copies = copies(0, mC, mL, mR)
    f_copies = copies(1, fC, fL, fR)
    w_copies = copies(2, wC, wL, wR)
    s_copies = copies(3, sC, sL, sR)
    start(m_copies)

    fC[0:depth, HALO : HALO + rows, :] = fix_ref[...]
    for r in range(rows // BX):
        for c in range(cols // BY):
            value = tis_ref[r, c].astype(F32)
            fC[depth, HALO + r * BX : HALO + (r + 1) * BX, c * BY : (c + 1) * BY] = jnp.full(
                (BX, BY), value, F32
            ).astype(BF16)
    start(f_copies)

    clear(mC, mL, mR)
    clear(fC, fL, fR)
    clear(wC, wL, wR)
    clear(sC, sL, sR)

    ki = lax.broadcasted_iota(jnp.int32, (wide, wide), 0)
    ji = lax.broadcasted_iota(jnp.int32, (wide, wide), 1)
    dist = jnp.abs(ki - ji)
    dist = jnp.minimum(dist, wide - dist)
    by_ref[...] = jnp.where(dist <= BOX, 1.0, 0.0).astype(BF16)
    size = GROUP * ext
    ki = lax.broadcasted_iota(jnp.int32, (size, size), 0)
    ji = lax.broadcasted_iota(jnp.int32, (size, size), 1)
    same = (ki // ext) == (ji // ext)
    bx_ref[...] = jnp.where(
        jnp.logical_and(same, jnp.abs(ki - ji) <= BOX), 1.0, 0.0
    ).astype(BF16)
    zpad = ZREACH + 1
    T[0:zpad] = jnp.zeros((zpad,) + T.shape[1:], F32)
    T[depth + zpad :] = jnp.zeros((zpad,) + T.shape[1:], F32)
    for k in range(5):
        Y[k, 0:BOX] = jnp.zeros((BOX, ext, wide), F32)
        Y[k, depth + BOX :] = jnp.zeros((BOX, ext, wide), F32)
    for k in range(3):
        A[k, 0:BOX] = jnp.zeros((BOX, ext, wide), F32)
        A[k, depth + BOX :] = jnp.zeros((BOX, ext, wide), F32)

    def side(left, right):
        lane = lax.broadcasted_iota(jnp.int32, left.shape, left.ndim - 1)
        return jnp.where(lane < BY // 2, right.astype(F32), left.astype(F32))

    def joined(center, left, right):
        s = side(left, right).astype(center.dtype)
        return jnp.concatenate([center, s], axis=-1)

    wait_recv(m_copies)
    vel_copy.wait()

    slab = BX + 2 * HALO
    for br in range(rows // BX):
        for bc in range(cols // BY):
            oz, ox, oy = off_ref[0, br, bc], off_ref[1, br, bc], off_ref[2, br, bc]
            lane = lax.broadcasted_iota(jnp.int32, (wide, 2 * BY), 1)
            target = jnp.where(lane < BY, lane, lane - BY + 1) + bc * BY + oy
            target = jnp.where(target < 0, target + wide, target)
            source = lax.broadcasted_iota(jnp.int32, (wide, 2 * BY), 0)
            shift = jnp.where(source == target, 1.0, 0.0).astype(BF16)
            r0 = br * BX
            i = lax.broadcasted_iota(jnp.int32, (GROUP * 2 * BX, GROUP * slab), 0)
            k = lax.broadcasted_iota(jnp.int32, (GROUP * 2 * BX, GROUP * slab), 1)
            row = (i // (2 * BX)) * slab + HALO + (i % BX) + (i // BX) % 2 + ox
            down = jnp.where(k == row, 1.0, 0.0).astype(BF16)

            def move(g, carry):
                z = pl.multiple_of(g * GROUP, GROUP)
                x = joined(
                    mC[pl.ds(z, GROUP), r0 : r0 + slab, :],
                    mL[pl.ds(z, GROUP), r0 : r0 + slab, :],
                    mR[pl.ds(z, GROUP), r0 : r0 + slab, :],
                )
                t = dot(x.reshape(GROUP * slab, wide), shift).astype(BF16)
                T[pl.ds(z + zpad, GROUP)] = dot(down, t).reshape(GROUP, 2 * BX, 2 * BY)
                return carry

            lax.fori_loop(0, depth // GROUP, move, 0)
            rs = slice(r0, r0 + BX)
            cs = slice(bc * BY, (bc + 1) * BY)
            hs = slice(HALO + r0, HALO + r0 + BX)

            def warp(z, carry):
                f0, f1, f2 = vel[0, z, rs, cs], vel[1, z, rs, cs], vel[2, z, rs, cs]
                planes, slopes_x, slopes_y = [], [], []
                for c in (0, 1):
                    vs, ds = [], []
                    for a in (0, 1):
                        s = T[z + zpad + oz + c, a * BX : (a + 1) * BX, :]
                        low, high = s[:, :BY], s[:, BY:]
                        d = high - low
                        vs.append((1.0 - f2) * low + f2 * high)
                        ds.append(d)
                    planes.append((1.0 - f1) * vs[0] + f1 * vs[1])
                    slopes_x.append(vs[1] - vs[0])
                    slopes_y.append((1.0 - f1) * ds[0] + f1 * ds[1])
                value = (1.0 - f0) * planes[0] + f0 * planes[1]
                wC[z, hs, cs] = value.astype(BF16)
                slopes = (
                    planes[1] - planes[0],
                    (1.0 - f0) * slopes_x[0] + f0 * slopes_x[1],
                    (1.0 - f0) * slopes_y[0] + f0 * slopes_y[1],
                )
                for k in range(3):
                    sF[k, z, rs, cs] = slopes[k]
                    sC[k * depth + z, hs, cs] = slopes[k].astype(BF16)
                return carry

            lax.fori_loop(0, depth, warp, 0)

    start(w_copies)
    start(s_copies)
    wait_recv(f_copies)
    wait_recv(w_copies)

    by = by_ref[...]

    def image(center, left, right, z):
        return joined(center[pl.ds(z, GROUP)], left[pl.ds(z, GROUP)], right[pl.ds(z, GROUP)])

    def stats_y(g, carry):
        z = g * GROUP
        i_low = image(wC, wL, wR, z).reshape(GROUP * ext, wide)
        j_low = image(fC, fL, fR, z).reshape(GROUP * ext, wide)
        i, j = i_low.astype(F32), j_low.astype(F32)
        fields = [(i_low,), (j_low,), split2(i * i), split2(j * j), split2(i * j)]
        for k, parts in enumerate(fields):
            y = dot(parts[0], by)
            for part in parts[1:]:
                y = y + dot(part, by)
            Y[k, pl.ds(z + BOX, GROUP)] = y.reshape(GROUP, ext, wide)
        return carry

    lax.fori_loop(0, depth // GROUP, stats_y, 0)

    def window_z(ref, k, z):
        p = [ref[k, z + t] for t in range(GROUP + 2 * BOX)]
        common = ((p[3] + p[4]) + (p[5] + p[6])) + (p[7] + p[8])
        low, high = p[1] + p[2], p[9] + p[10]
        outs = [
            common + (p[0] + low), common + (low + p[9]),
            common + (p[2] + high), common + (high + p[11]),
        ]
        return jnp.concatenate(outs, axis=0)

    mask = joined(fC[depth], fL[depth], fR[depth]).astype(F32)
    row = lax.broadcasted_iota(jnp.int32, (ext, wide), 0)
    lane = lax.broadcasted_iota(jnp.int32, (ext, wide), 1)
    own = jnp.logical_and(jnp.logical_and(row >= HALO, row < HALO + rows), lane < cols)
    own_mask = jnp.where(own, mask, 0.0)
    acc_ref[...] = jnp.zeros_like(acc_ref)

    def stats(g, carry):
        z = g * GROUP
        sums = []
        for k in range(5):
            h, m, l = split3(window_z(Y, k, z))
            sums.append(dot(bx_ref[...], h) + dot(bx_ref[...], m) + dot(bx_ref[...], l))
        si, sj, sii, sjj, sij = [s.reshape(GROUP, ext, wide) for s in sums]
        cross = sij - si * sj * (1.0 / COUNT)
        var_i = sii - si * si * (1.0 / COUNT)
        var_j = sjj - sj * sj * (1.0 / COUNT)
        q = cross / (var_i * var_j + EPS)
        live = mask[None] > 0.0
        acc_ref[...] += jnp.sum(jnp.where(own_mask[None] > 0.0, cross * q, 0.0), axis=0)
        q = jnp.where(live, q, 0.0)
        p = jnp.where(live, q * q * var_j, 0.0)
        terms = (
            jnp.where(live, (2.0 / COUNT) * (q * sj - p * si), 0.0), p, -2.0 * q,
        )
        for k in range(3):
            h, l = split2(terms[k].reshape(GROUP * ext, wide))
            y = dot(h, by_ref[...]) + dot(l, by_ref[...])
            A[k, pl.ds(z + BOX, GROUP)] = y.reshape(GROUP, ext, wide)
        return carry

    lax.fori_loop(0, depth // GROUP, stats, 0)

    wait_recv(s_copies)
    inner = slice(HALO - GHALO, HALO + rows + GHALO)

    def grads(g, carry):
        z = g * GROUP
        box = []
        for k in range(3):
            h, l = split2(window_z(A, k, z))
            b = dot(bx_ref[...], h) + dot(bx_ref[...], l)
            box.append(b.reshape(GROUP, ext, wide)[:, inner])
        i = image(wC, wL, wR, z).astype(F32)[:, inner]
        j = image(fC, fL, fR, z).astype(F32)[:, inner]
        grad = box[0] + 2.0 * i * box[1] + j * box[2]
        for k in range(3):
            zs = pl.ds(k * depth + z, GROUP)
            c = sC[zs].astype(F32)
            c = jnp.concatenate(
                [c[:, HALO - GHALO : HALO], sF[k, pl.ds(z, GROUP)],
                 c[:, HALO + rows : HALO + rows + GHALO]], axis=1)
            s = side(sL[zs], sR[zs])[:, inner]
            h, l = split2(grad * jnp.concatenate([c, s], axis=-1))
            gh_ref[k, pl.ds(z, GROUP)] = h
            gl_ref[k, pl.ds(z, GROUP)] = l
        return carry

    lax.fori_loop(0, depth // GROUP, grads, 0)
    for cs in (m_copies, f_copies, w_copies, s_copies):
        wait_send(cs)


def smooth_kernel(gh_ref, gl_ref, yh_ref, yl_ref, xh_ref, xl_ref, out_ref):
    _, depth, rows, wide = gh_ref.shape
    h = gh_ref[...].reshape(depth * rows, wide)
    l = gl_ref[...].reshape(depth * rows, wide)
    t = dot(h, yh_ref[...]) + dot(l, yh_ref[...]) + dot(h, yl_ref[...])
    h, l = split2(t)
    o = dot(xh_ref[...], h) + dot(xh_ref[...], l) + dot(xl_ref[...], h)
    out_ref[...] = o.reshape(out_ref.shape)


def gauss():
    taps = np.arange(-GAUSS_RADIUS, GAUSS_RADIUS + 1)
    w = np.exp(-(taps * taps) / (2.0 * GAUSS_SIGMA**2))
    return w / w.sum()


def as_pair(m):
    h = m.astype(jnp.bfloat16)
    return h, (m - h.astype(np.float64)).astype(jnp.bfloat16)


def gauss_y(cols):
    w, wide = gauss(), cols + BY
    m = np.zeros((wide, cols))
    for j in range(cols):
        for t in range(-GAUSS_RADIUS, GAUSS_RADIUS + 1):
            m[(j + t) % wide, j] = w[t + GAUSS_RADIUS]
    return as_pair(m)


def gauss_zx(depth, rows):
    w = gauss()
    mx = np.zeros((rows, rows + 2 * GHALO))
    mz = np.zeros((depth, depth))
    for t in range(-GAUSS_RADIUS, GAUSS_RADIUS + 1):
        for r in range(rows):
            mx[r, r + GHALO + t] = w[t + GAUSS_RADIUS]
        for z in range(depth):
            if 0 <= z + t < depth:
                mz[z, z + t] = w[t + GAUSS_RADIUS]
    return as_pair(-STEP_RATE * np.kron(mz, mx))


def on_device(nx, ny, moving, fixed, velocity, offsets, tissue):
    depth, rows, cols = moving.shape
    ext, wide, gext = rows + 2 * HALO, cols + BY, rows + 2 * GHALO

    def ring(n):
        return [
            pltpu.VMEM((n, ext, cols), BF16),
            pltpu.VMEM((n, ext, BY), BF16),
            pltpu.VMEM((n, ext, BY), BF16),
        ]

    vmem = pl.BlockSpec(memory_space=pltpu.VMEM)
    smem = pl.BlockSpec(memory_space=pltpu.SMEM)
    gshape = jax.ShapeDtypeStruct((3, depth, gext, wide), BF16)
    gh, gl, acc = pl.pallas_call(
        functools.partial(fused_kernel, nx, ny),
        out_shape=(gshape, gshape, jax.ShapeDtypeStruct((ext, wide), F32)),
        in_specs=[smem, smem, vmem, vmem, pl.BlockSpec(memory_space=pl.ANY)],
        out_specs=(vmem, vmem, vmem),
        scratch_shapes=[
            *ring(depth), *ring(depth + 1), *ring(depth), *ring(3 * depth),
            pltpu.VMEM(velocity.shape, F32),
            pltpu.VMEM((3, depth, rows, cols), F32),
            pltpu.VMEM((depth + 2 * (ZREACH + 1), 2 * BX, 2 * BY), F32),
            pltpu.VMEM((5, depth + 2 * BOX, ext, wide), F32),
            pltpu.VMEM((3, depth + 2 * BOX, ext, wide), F32),
            pltpu.VMEM((wide, wide), BF16),
            pltpu.VMEM((GROUP * ext, GROUP * ext), BF16),
            pltpu.SemaphoreType.DMA,
            pltpu.SemaphoreType.DMA((4, 8)),
            pltpu.SemaphoreType.DMA((4, 8)),
        ],
        compiler_params=pltpu.CompilerParams(
            collective_id=0, has_side_effects=True, vmem_limit_bytes=56 * 2**20
        ),
    )(offsets, tissue, moving, fixed, velocity)
    totals = lax.psum(
        jnp.stack([jnp.sum(acc), jnp.sum(tissue).astype(F32)]), ("gx", "gy")
    )
    loss = -totals[0] / (totals[1] * float(BX * BY * depth))

    yh, yl = gauss_y(cols)
    xh, xl = gauss_zx(depth, rows)
    gspec = pl.BlockSpec((1, depth, gext, wide), lambda k: (k, 0, 0, 0))
    whole = lambda a: pl.BlockSpec(a.shape, lambda k: (0, 0))
    update = pl.pallas_call(
        smooth_kernel,
        grid=(3,),
        out_shape=jax.ShapeDtypeStruct((3, depth, rows, cols), F32),
        in_specs=[gspec, gspec, whole(yh), whole(yl), whole(xh), whole(xl)],
        out_specs=pl.BlockSpec((1, depth, rows, cols), lambda k: (k, 0, 0, 0)),
        compiler_params=pltpu.CompilerParams(vmem_limit_bytes=48 * 2**20),
    )(gh, gl, jnp.asarray(yh), jnp.asarray(yl), jnp.asarray(xh), jnp.asarray(xl))
    return update, loss


def solution(mesh):
    in_specs = (
        P(None, "gx", "gy"),
        P(None, "gx", "gy"),
        P(None, None, "gx", "gy"),
        P(None, "gx", "gy"),
        P("gx", "gy"),
    )
    out_specs = (P(None, None, "gx", "gy"), P())
    return jax.shard_map(
        functools.partial(on_device, mesh.shape["gx"], mesh.shape["gy"]),
        mesh=mesh, in_specs=in_specs, out_specs=out_specs, check_vma=False,
    )
```

```python
import functools
import math

import jax
import jax.numpy as jnp
import numpy as np
from jax import lax
from jax.experimental import pallas as pl
from jax.experimental.pallas import tpu as pltpu
from jax.sharding import PartitionSpec as P

BX = 16
BY = 128
ZREACH = 2
BOX = 4
GAUSS_RADIUS = 7
GAUSS_SIGMA = 3.0
COUNT = 729.0
EPS = 1e-05
STEP_RATE = 16.0
HALO = 16
GHALO = 8
GROUP = 4
F32 = jnp.float32
BF16 = jnp.bfloat16
MESH = pl.DeviceIdType.MESH

DIRS = [(-1, 0), (1, 0), (0, -1), (0, 1), (-1, -1), (-1, 1), (1, -1), (1, 1)]


def dot(a, b):
    return jnp.dot(a, b, preferred_element_type=F32)


def split2(x):
    h = x.astype(BF16)
    return h, (x - h.astype(F32)).astype(BF16)


def split3(x):
    h = x.astype(BF16)
    r = x - h.astype(F32)
    m = r.astype(BF16)
    return h, m, (r - m.astype(F32)).astype(BF16)


def halo_refs(direction, rows, center, left, right):
    dx, dy = direction
    src_rows = {-1: pl.ds(HALO, HALO), 0: pl.ds(HALO, rows), 1: pl.ds(rows, HALO)}[dx]
    dst_rows = {-1: pl.ds(HALO + rows, HALO), 0: pl.ds(HALO, rows), 1: pl.ds(0, HALO)}[dx]
    cols = center.shape[2]
    if dy == 0:
        return center.at[:, src_rows, :], center.at[:, dst_rows, :]
    if dy < 0:
        return center.at[:, src_rows, pl.ds(0, BY)], right.at[:, dst_rows, :]
    return center.at[:, src_rows, pl.ds(cols - BY, BY)], left.at[:, dst_rows, :]


def fused_kernel(
    nx, ny,
    off_ref, tis_ref, mov_ref, fix_ref, vel_hbm, yh_hbm, yl_hbm, xh_hbm, xl_hbm,
    out_hbm, loss_ref,
    mC, mL, mR, fC, fL, fR, wC, wL, wR, sC, sL, sR,
    vel, sF, T, Y, A, by_ref, bx_ref,
    gh_ref, gl_ref, out, yh, yl, xh, xl, acc_ref, part, by_y, by_x,
    vel_sem, const_sem, out_sem, send_sem, recv_sem, ysend_sem, yrecv_sem, xsend_sem, xrecv_sem,
):
    depth, rows, cols = mov_ref.shape
    ext = rows + 2 * HALO
    wide = cols + BY
    gx, gy = lax.axis_index("gx"), lax.axis_index("gy")

    def exists(d):
        dx, dy = d
        c = None
        for cond in (
            (gx > 0) if dx < 0 else (gx < nx - 1) if dx > 0 else None,
            (gy > 0) if dy < 0 else (gy < ny - 1) if dy > 0 else None,
        ):
            if cond is not None:
                c = cond if c is None else jnp.logical_and(c, cond)
        return c

    has = [exists(d) for d in DIRS]

    vel_copy = pltpu.make_async_copy(vel_hbm, vel, vel_sem)
    vel_copy.start()
    const_copies = [
        pltpu.make_async_copy(a, b, const_sem.at[i])
        for i, (a, b) in enumerate(((yh_hbm, yh), (yl_hbm, yl), (xh_hbm, xh), (xl_hbm, xl)))
    ]
    for c in const_copies:
        c.start()

    barrier = pltpu.get_barrier_semaphore()
    for i, (dx, dy) in enumerate(DIRS):
        @pl.when(has[i])
        def _():
            pl.semaphore_signal(barrier, inc=1, device_id=(gx + dx, gy + dy), device_id_type=MESH)

    for d in range(1, ny):
        pl.semaphore_signal(
            barrier, inc=1, device_id=(gx, lax.rem(gy + d, ny)), device_id_type=MESH
        )
    for d in range(1, nx):
        pl.semaphore_signal(
            barrier, inc=1, device_id=(lax.rem(gx + d, nx), gy), device_id_type=MESH
        )

    def clear(center, left, right):
        for i, (dx, dy) in enumerate(DIRS):
            _, dst = halo_refs((-dx, -dy), rows, center, left, right)

            @pl.when(jnp.logical_not(has[i]))
            def _():
                dst[...] = jnp.zeros(dst.shape, dst.dtype)

    mC[:, HALO : HALO + rows, :] = mov_ref[...]
    def line(g, n):
        return 1 + jnp.where(g > 0, 1, 0) + jnp.where(g < n - 1, 1, 0)

    pl.semaphore_wait(barrier, line(gx, nx) * line(gy, ny) - 1 + (ny - 1) + (nx - 1))

    def copies(t, center, left, right):
        out = []
        for i, (dx, dy) in enumerate(DIRS):
            src, dst = halo_refs((dx, dy), rows, center, left, right)
            out.append(
                pltpu.make_async_remote_copy(
                    src_ref=src, dst_ref=dst,
                    send_sem=send_sem.at[t, i], recv_sem=recv_sem.at[t, i],
                    device_id=(gx + dx, gy + dy), device_id_type=MESH,
                )
            )
        return out

    def start(cs):
        for i, c in enumerate(cs):
            @pl.when(has[i])
            def _():
                c.start()

    def wait_recv(cs):
        for i, c in enumerate(cs):
            j = DIRS.index((-DIRS[i][0], -DIRS[i][1]))

            @pl.when(has[j])
            def _():
                c.wait_recv()

    def wait_send(cs):
        for i, c in enumerate(cs):
            @pl.when(has[i])
            def _():
                c.wait_send()

    m_copies = copies(0, mC, mL, mR)
    f_copies = copies(1, fC, fL, fR)
    w_copies = copies(2, wC, wL, wR)
    s_copies = copies(3, sC, sL, sR)
    start(m_copies)

    fC[0:depth, HALO : HALO + rows, :] = fix_ref[...]
    for r in range(rows // BX):
        for c in range(cols // BY):
            value = tis_ref[r, c].astype(F32)
            fC[depth, HALO + r * BX : HALO + (r + 1) * BX, c * BY : (c + 1) * BY] = jnp.full(
                (BX, BY), value, F32
            ).astype(BF16)
    start(f_copies)

    clear(mC, mL, mR)
    clear(fC, fL, fR)
    clear(wC, wL, wR)
    clear(sC, sL, sR)

    ki = lax.broadcasted_iota(jnp.int32, (wide, wide), 0)
    ji = lax.broadcasted_iota(jnp.int32, (wide, wide), 1)
    dist = jnp.abs(ki - ji)
    dist = jnp.minimum(dist, wide - dist)
    by_ref[...] = jnp.where(dist <= BOX, 1.0, 0.0).astype(BF16)
    size = GROUP * ext
    ki = lax.broadcasted_iota(jnp.int32, (size, size), 0)
    ji = lax.broadcasted_iota(jnp.int32, (size, size), 1)
    same = (ki // ext) == (ji // ext)
    bx_ref[...] = jnp.where(
        jnp.logical_and(same, jnp.abs(ki - ji) <= BOX), 1.0, 0.0
    ).astype(BF16)
    zpad = ZREACH + 1
    T[0:zpad] = jnp.zeros((zpad,) + T.shape[1:], F32)
    T[depth + zpad :] = jnp.zeros((zpad,) + T.shape[1:], F32)
    for k in range(5):
        Y[k, 0:BOX] = jnp.zeros((BOX, ext, wide), F32)
        Y[k, depth + BOX :] = jnp.zeros((BOX, ext, wide), F32)
    for k in range(3):
        A[k, 0:BOX] = jnp.zeros((BOX, ext, wide), F32)
        A[k, depth + BOX :] = jnp.zeros((BOX, ext, wide), F32)

    def side(left, right):
        lane = lax.broadcasted_iota(jnp.int32, left.shape, left.ndim - 1)
        return jnp.where(lane < BY // 2, right.astype(F32), left.astype(F32))

    def joined(center, left, right):
        s = side(left, right).astype(center.dtype)
        return jnp.concatenate([center, s], axis=-1)

    wait_recv(m_copies)
    vel_copy.wait()

    slab = BX + 2 * HALO
    for br in range(rows // BX):
        for bc in range(cols // BY):
            oz, ox, oy = off_ref[0, br, bc], off_ref[1, br, bc], off_ref[2, br, bc]
            lane = lax.broadcasted_iota(jnp.int32, (wide, 2 * BY), 1)
            target = jnp.where(lane < BY, lane, lane - BY + 1) + bc * BY + oy
            target = jnp.where(target < 0, target + wide, target)
            source = lax.broadcasted_iota(jnp.int32, (wide, 2 * BY), 0)
            shift = jnp.where(source == target, 1.0, 0.0).astype(BF16)
            r0 = br * BX
            i = lax.broadcasted_iota(jnp.int32, (GROUP * 2 * BX, GROUP * slab), 0)
            k = lax.broadcasted_iota(jnp.int32, (GROUP * 2 * BX, GROUP * slab), 1)
            row = (i // (2 * BX)) * slab + HALO + (i % BX) + (i // BX) % 2 + ox
            down = jnp.where(k == row, 1.0, 0.0).astype(BF16)

            def move(g, carry):
                z = pl.multiple_of(g * GROUP, GROUP)
                x = joined(
                    mC[pl.ds(z, GROUP), r0 : r0 + slab, :],
                    mL[pl.ds(z, GROUP), r0 : r0 + slab, :],
                    mR[pl.ds(z, GROUP), r0 : r0 + slab, :],
                )
                t = dot(x.reshape(GROUP * slab, wide), shift).astype(BF16)
                T[pl.ds(z + zpad, GROUP)] = dot(down, t).reshape(GROUP, 2 * BX, 2 * BY)
                return carry

            lax.fori_loop(0, depth // GROUP, move, 0)
            rs = slice(r0, r0 + BX)
            cs = slice(bc * BY, (bc + 1) * BY)
            hs = slice(HALO + r0, HALO + r0 + BX)

            def warp(z, carry):
                f0, f1, f2 = vel[0, z, rs, cs], vel[1, z, rs, cs], vel[2, z, rs, cs]
                planes, slopes_x, slopes_y = [], [], []
                for c in (0, 1):
                    vs, ds = [], []
                    for a in (0, 1):
                        s = T[z + zpad + oz + c, a * BX : (a + 1) * BX, :]
                        low, high = s[:, :BY], s[:, BY:]
                        d = high - low
                        vs.append((1.0 - f2) * low + f2 * high)
                        ds.append(d)
                    planes.append((1.0 - f1) * vs[0] + f1 * vs[1])
                    slopes_x.append(vs[1] - vs[0])
                    slopes_y.append((1.0 - f1) * ds[0] + f1 * ds[1])
                value = (1.0 - f0) * planes[0] + f0 * planes[1]
                wC[z, hs, cs] = value.astype(BF16)
                slopes = (
                    planes[1] - planes[0],
                    (1.0 - f0) * slopes_x[0] + f0 * slopes_x[1],
                    (1.0 - f0) * slopes_y[0] + f0 * slopes_y[1],
                )
                for k in range(3):
                    sF[k, z, rs, cs] = slopes[k]
                    sC[k * depth + z, hs, cs] = slopes[k].astype(BF16)
                return carry

            lax.fori_loop(0, depth, warp, 0)

    start(w_copies)
    start(s_copies)
    wait_recv(f_copies)
    wait_recv(w_copies)

    by = by_ref[...]

    def image(center, left, right, z):
        return joined(center[pl.ds(z, GROUP)], left[pl.ds(z, GROUP)], right[pl.ds(z, GROUP)])

    def stats_y(g, carry):
        z = g * GROUP
        i_low = image(wC, wL, wR, z).reshape(GROUP * ext, wide)
        j_low = image(fC, fL, fR, z).reshape(GROUP * ext, wide)
        i, j = i_low.astype(F32), j_low.astype(F32)
        fields = [(i_low,), (j_low,), split2(i * i), split2(j * j), split2(i * j)]
        for k, parts in enumerate(fields):
            y = dot(parts[0], by)
            for part in parts[1:]:
                y = y + dot(part, by)
            Y[k, pl.ds(z + BOX, GROUP)] = y.reshape(GROUP, ext, wide)
        return carry

    lax.fori_loop(0, depth // GROUP, stats_y, 0)

    def window_z(ref, k, z):
        p = [ref[k, z + t] for t in range(GROUP + 2 * BOX)]
        common = ((p[3] + p[4]) + (p[5] + p[6])) + (p[7] + p[8])
        low, high = p[1] + p[2], p[9] + p[10]
        outs = [
            common + (p[0] + low), common + (low + p[9]),
            common + (p[2] + high), common + (high + p[11]),
        ]
        return jnp.concatenate(outs, axis=0)

    mask = joined(fC[depth], fL[depth], fR[depth]).astype(F32)
    row = lax.broadcasted_iota(jnp.int32, (ext, wide), 0)
    lane = lax.broadcasted_iota(jnp.int32, (ext, wide), 1)
    own = jnp.logical_and(jnp.logical_and(row >= HALO, row < HALO + rows), lane < cols)
    own_mask = jnp.where(own, mask, 0.0)
    acc_ref[...] = jnp.zeros_like(acc_ref)

    def stats(g, carry):
        z = g * GROUP
        sums = []
        for k in range(5):
            h, m, l = split3(window_z(Y, k, z))
            sums.append(dot(bx_ref[...], h) + dot(bx_ref[...], m) + dot(bx_ref[...], l))
        si, sj, sii, sjj, sij = [s.reshape(GROUP, ext, wide) for s in sums]
        cross = sij - si * sj * (1.0 / COUNT)
        var_i = sii - si * si * (1.0 / COUNT)
        var_j = sjj - sj * sj * (1.0 / COUNT)
        q = cross / (var_i * var_j + EPS)
        live = mask[None] > 0.0
        acc_ref[...] += jnp.sum(jnp.where(own_mask[None] > 0.0, cross * q, 0.0), axis=0)
        q = jnp.where(live, q, 0.0)
        p = jnp.where(live, q * q * var_j, 0.0)
        terms = (
            jnp.where(live, (2.0 / COUNT) * (q * sj - p * si), 0.0), p, -2.0 * q,
        )
        for k in range(3):
            h, l = split2(terms[k].reshape(GROUP * ext, wide))
            y = dot(h, by_ref[...]) + dot(l, by_ref[...])
            A[k, pl.ds(z + BOX, GROUP)] = y.reshape(GROUP, ext, wide)
        return carry

    lax.fori_loop(0, depth // GROUP, stats, 0)

    def folded(x):
        x = sum(x[r : r + 8] for r in range(0, ext, 8))
        return sum(x[:, c : c + BY] for c in range(0, wide, BY))

    blocks = 0
    for r in range(rows // BX):
        for c in range(cols // BY):
            blocks = blocks + tis_ref[r, c]
    part[0, 0:8] = folded(acc_ref[...])
    part[0, 8:16] = jnp.full((8, BY), blocks.astype(F32), F32)

    def spread(n, axis_of, src, dst, ssem, rsem):
        return [
            pltpu.make_async_remote_copy(
                src_ref=src, dst_ref=dst.at[d], send_sem=ssem.at[d], recv_sem=rsem.at[d],
                device_id=axis_of(d), device_id_type=MESH,
            )
            for d in range(1, n)
        ]

    y_copies = spread(
        ny, lambda d: (gx, lax.rem(gy + d, ny)), part.at[0], by_y, ysend_sem, yrecv_sem
    )
    x_copies = spread(
        nx, lambda d: (lax.rem(gx + d, nx), gy), part.at[1], by_x, xsend_sem, xrecv_sem
    )
    for c in y_copies:
        c.start()

    wait_recv(s_copies)
    inner = slice(HALO - GHALO, HALO + rows + GHALO)

    def grads(g, carry):
        z = g * GROUP
        box = []
        for k in range(3):
            h, l = split2(window_z(A, k, z))
            b = dot(bx_ref[...], h) + dot(bx_ref[...], l)
            box.append(b.reshape(GROUP, ext, wide)[:, inner])
        i = image(wC, wL, wR, z).astype(F32)[:, inner]
        j = image(fC, fL, fR, z).astype(F32)[:, inner]
        grad = box[0] + 2.0 * i * box[1] + j * box[2]
        for k in range(3):
            zs = pl.ds(k * depth + z, GROUP)
            c = sC[zs].astype(F32)
            c = jnp.concatenate(
                [c[:, HALO - GHALO : HALO], sF[k, pl.ds(z, GROUP)],
                 c[:, HALO + rows : HALO + rows + GHALO]], axis=1)
            s = side(sL[zs], sR[zs])[:, inner]
            h, l = split2(grad * jnp.concatenate([c, s], axis=-1))
            gh_ref[k, pl.ds(z, GROUP)] = h
            gl_ref[k, pl.ds(z, GROUP)] = l
        return carry

    lax.fori_loop(0, depth // GROUP, grads, 0)

    for c in y_copies:
        c.wait()
    total = part[0]
    for d in range(1, ny):
        total = total + by_y[d]
    part[1] = total
    for c in x_copies:
        c.start()

    for c in const_copies:
        c.wait()
    out_copies = []
    for k in range(3):
        h = gh_ref[k].reshape(depth * (rows + 2 * GHALO), wide)
        l = gl_ref[k].reshape(depth * (rows + 2 * GHALO), wide)
        t = dot(h, yh[...]) + dot(l, yh[...]) + dot(h, yl[...])
        h, l = split2(t)
        o = dot(xh[...], h) + dot(xh[...], l) + dot(xl[...], h)
        out[k] = o.reshape(depth, rows, cols)
        copy = pltpu.make_async_copy(out.at[k], out_hbm.at[k], out_sem.at[k])
        copy.start()
        out_copies.append(copy)

    for c in x_copies:
        c.wait()
    total = part[1]
    for d in range(1, nx):
        total = total + by_x[d]
    tissue_total = jnp.max(total[8:16], keepdims=True)
    loss_ref[...] = -jnp.sum(total[0:8], keepdims=True) / (
        tissue_total * float(BX * BY * depth)
    )
    for c in out_copies:
        c.wait()
    for cs in (m_copies, f_copies, w_copies, s_copies):
        wait_send(cs)


def gauss():
    taps = np.arange(-GAUSS_RADIUS, GAUSS_RADIUS + 1)
    w = np.exp(-(taps * taps) / (2.0 * GAUSS_SIGMA**2))
    return w / w.sum()


def as_pair(m):
    h = m.astype(jnp.bfloat16)
    return h, (m - h.astype(np.float64)).astype(jnp.bfloat16)


def gauss_y(cols):
    w, wide = gauss(), cols + BY
    m = np.zeros((wide, cols))
    for j in range(cols):
        for t in range(-GAUSS_RADIUS, GAUSS_RADIUS + 1):
            m[(j + t) % wide, j] = w[t + GAUSS_RADIUS]
    return as_pair(m)


def gauss_zx(depth, rows):
    w = gauss()
    mx = np.zeros((rows, rows + 2 * GHALO))
    mz = np.zeros((depth, depth))
    for t in range(-GAUSS_RADIUS, GAUSS_RADIUS + 1):
        for r in range(rows):
            mx[r, r + GHALO + t] = w[t + GAUSS_RADIUS]
        for z in range(depth):
            if 0 <= z + t < depth:
                mz[z, z + t] = w[t + GAUSS_RADIUS]
    return as_pair(-STEP_RATE * np.kron(mz, mx))


def on_device(nx, ny, moving, fixed, velocity, offsets, tissue):
    depth, rows, cols = moving.shape
    ext, wide, gext = rows + 2 * HALO, cols + BY, rows + 2 * GHALO

    def ring(n):
        return [
            pltpu.VMEM((n, ext, cols), BF16),
            pltpu.VMEM((n, ext, BY), BF16),
            pltpu.VMEM((n, ext, BY), BF16),
        ]

    vmem = pl.BlockSpec(memory_space=pltpu.VMEM)
    smem = pl.BlockSpec(memory_space=pltpu.SMEM)
    gshape = (3, depth, gext, wide)
    hbm = pl.BlockSpec(memory_space=pl.ANY)
    consts = gauss_y(cols) + gauss_zx(depth, rows)
    update, loss = pl.pallas_call(
        functools.partial(fused_kernel, nx, ny),
        out_shape=(
            jax.ShapeDtypeStruct((3, depth, rows, cols), F32),
            jax.ShapeDtypeStruct((1, 1), F32),
        ),
        in_specs=[smem, smem, vmem, vmem, hbm, hbm, hbm, hbm, hbm],
        out_specs=(hbm, vmem),
        scratch_shapes=[
            *ring(depth), *ring(depth + 1), *ring(depth), *ring(3 * depth),
            pltpu.VMEM(velocity.shape, F32),
            pltpu.VMEM((3, depth, rows, cols), F32),
            pltpu.VMEM((depth + 2 * (ZREACH + 1), 2 * BX, 2 * BY), F32),
            pltpu.VMEM((5, depth + 2 * BOX, ext, wide), F32),
            pltpu.VMEM((3, depth + 2 * BOX, ext, wide), F32),
            pltpu.VMEM((wide, wide), BF16),
            pltpu.VMEM((GROUP * ext, GROUP * ext), BF16),
            pltpu.VMEM(gshape, BF16),
            pltpu.VMEM(gshape, BF16),
            pltpu.VMEM((3, depth, rows, cols), F32),
            *[pltpu.VMEM(c.shape, BF16) for c in consts],
            pltpu.VMEM((ext, wide), F32),
            pltpu.VMEM((2, 16, BY), F32),
            pltpu.VMEM((ny, 16, BY), F32),
            pltpu.VMEM((nx, 16, BY), F32),
            pltpu.SemaphoreType.DMA,
            pltpu.SemaphoreType.DMA((4,)),
            pltpu.SemaphoreType.DMA((3,)),
            pltpu.SemaphoreType.DMA((4, 8)),
            pltpu.SemaphoreType.DMA((4, 8)),
            pltpu.SemaphoreType.DMA((ny,)),
            pltpu.SemaphoreType.DMA((ny,)),
            pltpu.SemaphoreType.DMA((nx,)),
            pltpu.SemaphoreType.DMA((nx,)),
        ],
        compiler_params=pltpu.CompilerParams(
            collective_id=0, has_side_effects=True, vmem_limit_bytes=56 * 2**20
        ),
    )(offsets, tissue, moving, fixed, velocity, *[jnp.asarray(c) for c in consts])
    return update, loss[0, 0]


def solution(mesh):
    in_specs = (
        P(None, "gx", "gy"),
        P(None, "gx", "gy"),
        P(None, None, "gx", "gy"),
        P(None, "gx", "gy"),
        P("gx", "gy"),
    )
    out_specs = (P(None, None, "gx", "gy"), P())
    return jax.shard_map(
        functools.partial(on_device, mesh.shape["gx"], mesh.shape["gy"]),
        mesh=mesh, in_specs=in_specs, out_specs=out_specs, check_vma=False,
    )
```

```python
import functools
import math

import jax
import jax.numpy as jnp
import numpy as np
from jax import lax
from jax.experimental import pallas as pl
from jax.experimental.pallas import tpu as pltpu
from jax.sharding import PartitionSpec as P

BX = 16
BY = 128
ZREACH = 2
BOX = 4
GAUSS_RADIUS = 7
GAUSS_SIGMA = 3.0
COUNT = 729.0
EPS = 1e-05
STEP_RATE = 16.0
HALO = 16
GHALO = 8
PACK = BY // HALO
GROUP = 4
F32 = jnp.float32
BF16 = jnp.bfloat16
MESH = pl.DeviceIdType.MESH

DIRS = [(-1, 0), (1, 0), (0, -1), (0, 1), (-1, -1), (-1, 1), (1, -1), (1, 1)]


def dot(a, b):
    return jnp.dot(a, b, preferred_element_type=F32)


def split2(x):
    h = x.astype(BF16)
    return h, (x - h.astype(F32)).astype(BF16)


def split3(x):
    h = x.astype(BF16)
    r = x - h.astype(F32)
    m = r.astype(BF16)
    return h, m, (r - m.astype(F32)).astype(BF16)


def halo_refs(direction, rows, center, to_left, to_right, left, right):
    dx, dy = direction
    cols = center.shape[2] - BY
    dst_rows = {-1: pl.ds(HALO + rows, HALO), 0: pl.ds(HALO, rows), 1: pl.ds(0, HALO)}[dx]
    if dy == 0:
        src_rows = pl.ds(HALO, HALO) if dx < 0 else pl.ds(rows, HALO)
        own = pl.ds(0, cols)
        return center.at[:, src_rows, own], center.at[:, dst_rows, own]
    src_rows = {-1: pl.ds(0, HALO), 0: pl.ds(0, rows), 1: pl.ds(rows - HALO, HALO)}[dx]
    if dy < 0:
        return to_left.at[:, src_rows, :], right.at[:, dst_rows, :]
    return to_right.at[:, src_rows, :], left.at[:, dst_rows, :]


def groups_of(planes, body):
    def step(g, carry):
        body(g * PACK, g, PACK)
        return carry

    lax.fori_loop(0, planes // PACK, step, 0)
    if planes % PACK:
        body(planes - planes % PACK, planes // PACK, planes % PACK)


def turn(x, shift, axis):
    shift %= x.shape[axis]
    return x if shift == 0 else pltpu.roll(x, shift, axis)


def pack(center, to_left, to_right, rows):
    cols = center.shape[2] - BY
    lane = lax.broadcasted_iota(jnp.int32, (rows, BY), 1)

    def body(z, g, count):
        l = jnp.zeros((rows, BY), F32)
        r = jnp.zeros((rows, BY), F32)
        for i in range(count):
            mine = jnp.logical_and(lane >= i * HALO, lane < (i + 1) * HALO)
            a = center[z + i, HALO : HALO + rows, 0:BY].astype(F32)
            b = center[z + i, HALO : HALO + rows, cols - BY : cols].astype(F32)
            l = jnp.where(mine, turn(a, i * HALO, 1), l)
            r = jnp.where(mine, turn(b, (i + 1) * HALO, 1), r)
        to_left[g] = l.astype(BF16)
        to_right[g] = r.astype(BF16)

    groups_of(center.shape[0], body)


def unpack(center, left, right):
    _, ext, wide = center.shape
    lane = lax.broadcasted_iota(jnp.int32, (ext, BY), 1)

    def body(z, g, count):
        l, r = left[g].astype(F32), right[g].astype(F32)
        for i in range(count):
            v = jnp.where(lane < HALO, turn(r, -i * HALO, 1), 0.0)
            v = jnp.where(lane >= BY - HALO, turn(l, -(i + 1) * HALO, 1), v)
            center[z + i, :, wide - BY : wide] = v.astype(BF16)

    groups_of(center.shape[0], body)


def window_x(v):
    s = v + turn(v, 1, 0) + turn(v, -1, 0)
    return s + turn(s, 3, 0) + turn(s, -3, 0)


def fused_kernel(
    nx, ny,
    off_ref, tis_ref, mov_ref, fix_ref, vel_hbm, yh_hbm, yl_hbm, xh_hbm, xl_hbm,
    out_hbm, loss_ref,
    m, f, w, s,
    vel, sF, T, Y, A, by_ref,
    gh_ref, gl_ref, out, yh, yl, xh, xl, acc_ref, mask_ref, own_ref, part, by_y, by_x,
    vel_sem, const_sem, out_sem, send_sem, recv_sem, ysend_sem, yrecv_sem, xsend_sem, xrecv_sem,
):
    (mC, fC, wC, sC) = (m[0], f[0], w[0], s[0])
    depth, rows, cols = mov_ref.shape
    ext = rows + 2 * HALO
    wide = cols + BY
    gx, gy = lax.axis_index("gx"), lax.axis_index("gy")

    def exists(d):
        dx, dy = d
        c = None
        for cond in (
            (gx > 0) if dx < 0 else (gx < nx - 1) if dx > 0 else None,
            (gy > 0) if dy < 0 else (gy < ny - 1) if dy > 0 else None,
        ):
            if cond is not None:
                c = cond if c is None else jnp.logical_and(c, cond)
        return c

    has = [exists(d) for d in DIRS]

    vel_copy = pltpu.make_async_copy(vel_hbm, vel, vel_sem)
    vel_copy.start()
    const_copies = [
        pltpu.make_async_copy(a, b, const_sem.at[i])
        for i, (a, b) in enumerate(((yh_hbm, yh), (yl_hbm, yl), (xh_hbm, xh), (xl_hbm, xl)))
    ]
    for c in const_copies:
        c.start()

    barrier = pltpu.get_barrier_semaphore()
    for i, (dx, dy) in enumerate(DIRS):
        @pl.when(has[i])
        def _():
            pl.semaphore_signal(barrier, inc=1, device_id=(gx + dx, gy + dy), device_id_type=MESH)

    for d in range(1, ny):
        pl.semaphore_signal(
            barrier, inc=1, device_id=(gx, lax.rem(gy + d, ny)), device_id_type=MESH
        )
    for d in range(1, nx):
        pl.semaphore_signal(
            barrier, inc=1, device_id=(lax.rem(gx + d, nx), gy), device_id_type=MESH
        )

    def clear(*bufs):
        for i, (dx, dy) in enumerate(DIRS):
            _, dst = halo_refs((-dx, -dy), rows, *bufs)

            @pl.when(jnp.logical_not(has[i]))
            def _():
                dst[...] = jnp.zeros(dst.shape, dst.dtype)

    mC[:, HALO : HALO + rows, 0:cols] = mov_ref[...]
    pack(m[0], m[1], m[2], rows)
    def line(g, n):
        return 1 + jnp.where(g > 0, 1, 0) + jnp.where(g < n - 1, 1, 0)

    pl.semaphore_wait(barrier, line(gx, nx) * line(gy, ny) - 1 + (ny - 1) + (nx - 1))

    def copies(t, *bufs):
        out = []
        for i, (dx, dy) in enumerate(DIRS):
            src, dst = halo_refs((dx, dy), rows, *bufs)
            out.append(
                pltpu.make_async_remote_copy(
                    src_ref=src, dst_ref=dst,
                    send_sem=send_sem.at[t, i], recv_sem=recv_sem.at[t, i],
                    device_id=(gx + dx, gy + dy), device_id_type=MESH,
                )
            )
        return out

    def start(cs):
        for i, c in enumerate(cs):
            @pl.when(has[i])
            def _():
                c.start()

    def wait_recv(cs):
        for i, c in enumerate(cs):
            j = DIRS.index((-DIRS[i][0], -DIRS[i][1]))

            @pl.when(has[j])
            def _():
                c.wait_recv()

    def wait_send(cs):
        for i, c in enumerate(cs):
            @pl.when(has[i])
            def _():
                c.wait_send()

    m_copies = copies(0, *m)
    f_copies = copies(1, *f)
    w_copies = copies(2, *w)
    s_copies = copies(3, *s)
    start(m_copies)

    fC[0:depth, HALO : HALO + rows, 0:cols] = fix_ref[...]
    for r in range(rows // BX):
        for c in range(cols // BY):
            value = tis_ref[r, c].astype(F32)
            fC[depth, HALO + r * BX : HALO + (r + 1) * BX, c * BY : (c + 1) * BY] = jnp.full(
                (BX, BY), value, F32
            ).astype(BF16)
    pack(f[0], f[1], f[2], rows)
    start(f_copies)

    clear(*m)
    clear(*f)
    clear(*w)
    clear(*s)

    ki = lax.broadcasted_iota(jnp.int32, (wide, wide), 0)
    ji = lax.broadcasted_iota(jnp.int32, (wide, wide), 1)
    dist = jnp.abs(ki - ji)
    dist = jnp.minimum(dist, wide - dist)
    by_ref[...] = jnp.where(dist <= BOX, 1.0, 0.0).astype(BF16)
    zpad = ZREACH + 1
    T[0:zpad] = jnp.zeros((zpad,) + T.shape[1:], F32)
    T[depth + zpad :] = jnp.zeros((zpad,) + T.shape[1:], F32)
    for k in range(5):
        Y[k, 0:BOX] = jnp.zeros((BOX, ext, wide), F32)
        Y[k, depth + BOX :] = jnp.zeros((BOX, ext, wide), F32)
    for k in range(3):
        A[k, 0:BOX] = jnp.zeros((BOX, ext, wide), F32)
        A[k, depth + BOX :] = jnp.zeros((BOX, ext, wide), F32)

    wait_recv(m_copies)
    unpack(m[0], m[3], m[4])
    vel_copy.wait()

    slab = BX + 2 * HALO
    for br in range(rows // BX):
        for bc in range(cols // BY):
            oz, ox, oy = off_ref[0, br, bc], off_ref[1, br, bc], off_ref[2, br, bc]
            lane = lax.broadcasted_iota(jnp.int32, (wide, 2 * BY), 1)
            target = jnp.where(lane < BY, lane, lane - BY + 1) + bc * BY + oy
            target = jnp.where(target < 0, target + wide, target)
            source = lax.broadcasted_iota(jnp.int32, (wide, 2 * BY), 0)
            shift = jnp.where(source == target, 1.0, 0.0).astype(BF16)
            r0 = br * BX
            i = lax.broadcasted_iota(jnp.int32, (GROUP * 2 * BX, GROUP * slab), 0)
            k = lax.broadcasted_iota(jnp.int32, (GROUP * 2 * BX, GROUP * slab), 1)
            row = (i // (2 * BX)) * slab + HALO + (i % BX) + (i // BX) % 2 + ox
            down = jnp.where(k == row, 1.0, 0.0).astype(BF16)

            def move(g, carry):
                z = pl.multiple_of(g * GROUP, GROUP)
                x = mC[pl.ds(z, GROUP), r0 : r0 + slab, :]
                t = dot(x.reshape(GROUP * slab, wide), shift).astype(BF16)
                T[pl.ds(z + zpad, GROUP)] = dot(down, t).reshape(GROUP, 2 * BX, 2 * BY)
                return carry

            lax.fori_loop(0, depth // GROUP, move, 0)
            rs = slice(r0, r0 + BX)
            cs = slice(bc * BY, (bc + 1) * BY)
            hs = slice(HALO + r0, HALO + r0 + BX)

            def warp(z, carry):
                f0, f1, f2 = vel[0, z, rs, cs], vel[1, z, rs, cs], vel[2, z, rs, cs]
                planes, slopes_x, slopes_y = [], [], []
                for c in (0, 1):
                    vs, ds = [], []
                    for a in (0, 1):
                        s = T[z + zpad + oz + c, a * BX : (a + 1) * BX, :]
                        low, high = s[:, :BY], s[:, BY:]
                        d = high - low
                        vs.append((1.0 - f2) * low + f2 * high)
                        ds.append(d)
                    planes.append((1.0 - f1) * vs[0] + f1 * vs[1])
                    slopes_x.append(vs[1] - vs[0])
                    slopes_y.append((1.0 - f1) * ds[0] + f1 * ds[1])
                value = (1.0 - f0) * planes[0] + f0 * planes[1]
                wC[z, hs, cs] = value.astype(BF16)
                slopes = (
                    planes[1] - planes[0],
                    (1.0 - f0) * slopes_x[0] + f0 * slopes_x[1],
                    (1.0 - f0) * slopes_y[0] + f0 * slopes_y[1],
                )
                for k in range(3):
                    sF[k, z, rs, cs] = slopes[k]
                    sC[k * depth + z, hs, cs] = slopes[k].astype(BF16)
                return carry

            lax.fori_loop(0, depth, warp, 0)

    pack(w[0], w[1], w[2], rows)
    start(w_copies)
    pack(s[0], s[1], s[2], rows)
    start(s_copies)
    wait_recv(f_copies)
    unpack(f[0], f[3], f[4])

    by = by_ref[...]

    def fixed_y(g, carry):
        z = g * GROUP
        j_low = fC[pl.ds(z, GROUP)].reshape(GROUP * ext, wide)
        j = j_low.astype(F32)
        h, l = split2(j * j)
        Y[1, pl.ds(z + BOX, GROUP)] = dot(j_low, by).reshape(GROUP, ext, wide)
        Y[3, pl.ds(z + BOX, GROUP)] = (dot(h, by) + dot(l, by)).reshape(GROUP, ext, wide)
        return carry

    lax.fori_loop(0, depth // GROUP, fixed_y, 0)
    wait_recv(w_copies)
    unpack(w[0], w[3], w[4])

    def stats_y(g, carry):
        z = g * GROUP
        i_low = wC[pl.ds(z, GROUP)].reshape(GROUP * ext, wide)
        i = i_low.astype(F32)
        j = fC[pl.ds(z, GROUP)].reshape(GROUP * ext, wide).astype(F32)
        fields = [(0, (i_low,)), (2, split2(i * i)), (4, split2(i * j))]
        for k, parts in fields:
            y = dot(parts[0], by)
            for part in parts[1:]:
                y = y + dot(part, by)
            Y[k, pl.ds(z + BOX, GROUP)] = y.reshape(GROUP, ext, wide)
        return carry

    lax.fori_loop(0, depth // GROUP, stats_y, 0)

    def window_z(ref, k, z, tile):
        p = [ref[k, z + t, :, tile] for t in range(GROUP + 2 * BOX)]
        common = ((p[3] + p[4]) + (p[5] + p[6])) + (p[7] + p[8])
        low, high = p[1] + p[2], p[9] + p[10]
        outs = [
            common + (p[0] + low), common + (low + p[9]),
            common + (p[2] + high), common + (high + p[11]),
        ]
        return window_x(jnp.concatenate(outs, axis=0))

    tiles = [slice(c, c + BY) for c in range(0, wide, BY)]

    row = lax.broadcasted_iota(jnp.int32, (ext, wide), 0)
    lane = lax.broadcasted_iota(jnp.int32, (ext, wide), 1)
    own_row = jnp.logical_and(row >= HALO, row < HALO + rows)
    acc_ref[...] = jnp.zeros_like(acc_ref)
    reach = HALO - BOX - 1
    near = jnp.logical_and(row >= HALO - reach, row < HALO + rows + reach)
    near = jnp.logical_and(near, jnp.logical_or(lane < cols + reach, lane >= wide - reach))
    mask_ref[...] = jnp.where(near, fC[depth].astype(F32), 0.0)
    own_ref[...] = jnp.where(jnp.logical_and(own_row, lane < cols), mask_ref[...], 0.0)

    def stats(g, carry):
        z = g * GROUP
        terms = [[], [], []]
        for tile in tiles:
            si, sj, sii, sjj, sij = [
                window_z(Y, k, z, tile).reshape(GROUP, ext, BY) for k in range(5)
            ]
            cross = sij - si * sj * (1.0 / COUNT)
            var_i = sii - si * si * (1.0 / COUNT)
            var_j = sjj - sj * sj * (1.0 / COUNT)
            q = cross / (var_i * var_j + EPS)
            live = mask_ref[:, tile][None] > 0.0
            if tile.start < cols:
                own = own_ref[:, tile][None] > 0.0
                acc_ref[:, tile] += jnp.sum(jnp.where(own, cross * q, 0.0), axis=0)
            q = jnp.where(live, q, 0.0)
            p = q * q * var_j
            values = ((2.0 / COUNT) * (q * sj - p * si), p, -2.0 * q)
            for k in range(3):
                terms[k].append(values[k].reshape(GROUP * ext, BY))
        for k in range(3):
            h, l = split2(jnp.concatenate(terms[k], axis=1))
            y = dot(h, by_ref[...]) + dot(l, by_ref[...])
            A[k, pl.ds(z + BOX, GROUP)] = y.reshape(GROUP, ext, wide)
        return carry

    lax.fori_loop(0, depth // GROUP, stats, 0)

    def folded(x):
        x = sum(x[r : r + 8] for r in range(0, ext, 8))
        return sum(x[:, c : c + BY] for c in range(0, wide, BY))

    blocks = 0
    for r in range(rows // BX):
        for c in range(cols // BY):
            blocks = blocks + tis_ref[r, c]
    part[0, 0:8] = folded(acc_ref[...])
    part[0, 8:16] = jnp.full((8, BY), blocks.astype(F32), F32)

    def spread(n, axis_of, src, dst, ssem, rsem):
        return [
            pltpu.make_async_remote_copy(
                src_ref=src, dst_ref=dst.at[d], send_sem=ssem.at[d], recv_sem=rsem.at[d],
                device_id=axis_of(d), device_id_type=MESH,
            )
            for d in range(1, n)
        ]

    y_copies = spread(
        ny, lambda d: (gx, lax.rem(gy + d, ny)), part.at[0], by_y, ysend_sem, yrecv_sem
    )
    x_copies = spread(
        nx, lambda d: (lax.rem(gx + d, nx), gy), part.at[1], by_x, xsend_sem, xrecv_sem
    )
    for c in y_copies:
        c.start()

    wait_recv(s_copies)
    unpack(s[0], s[3], s[4])
    inner = slice(HALO - GHALO, HALO + rows + GHALO)

    def grads(g, carry):
        z = g * GROUP
        for tile in tiles:
            box = [
                window_z(A, k, z, tile).reshape(GROUP, ext, BY)[:, inner] for k in range(3)
            ]
            i = wC[pl.ds(z, GROUP), :, tile].astype(F32)[:, inner]
            j = fC[pl.ds(z, GROUP), :, tile].astype(F32)[:, inner]
            grad = box[0] + 2.0 * i * box[1] + j * box[2]
            for k in range(3):
                c = sC[pl.ds(k * depth + z, GROUP), :, tile].astype(F32)
                if tile.start < cols:
                    c = jnp.concatenate(
                        [c[:, HALO - GHALO : HALO], sF[k, pl.ds(z, GROUP), :, tile],
                         c[:, HALO + rows : HALO + rows + GHALO]], axis=1)
                else:
                    c = c[:, inner]
                h, l = split2(grad * c)
                gh_ref[k, pl.ds(z, GROUP), :, tile] = h
                gl_ref[k, pl.ds(z, GROUP), :, tile] = l
        return carry

    lax.fori_loop(0, depth // GROUP, grads, 0)

    for c in y_copies:
        c.wait()
    total = part[0]
    for d in range(1, ny):
        total = total + by_y[d]
    part[1] = total
    for c in x_copies:
        c.start()

    for c in const_copies:
        c.wait()
    out_copies = []
    for k in range(3):
        h = gh_ref[k].reshape(depth * (rows + 2 * GHALO), wide)
        l = gl_ref[k].reshape(depth * (rows + 2 * GHALO), wide)
        t = dot(h, yh[...]) + dot(l, yh[...]) + dot(h, yl[...])
        h, l = split2(t)
        o = dot(xh[...], h) + dot(xh[...], l) + dot(xl[...], h)
        out[k] = o.reshape(depth, rows, cols)
        copy = pltpu.make_async_copy(out.at[k], out_hbm.at[k], out_sem.at[k])
        copy.start()
        out_copies.append(copy)

    for c in x_copies:
        c.wait()
    total = part[1]
    for d in range(1, nx):
        total = total + by_x[d]
    tissue_total = jnp.max(total[8:16], keepdims=True)
    loss_ref[...] = -jnp.sum(total[0:8], keepdims=True) / (
        tissue_total * float(BX * BY * depth)
    )
    for c in out_copies:
        c.wait()
    for cs in (m_copies, f_copies, w_copies, s_copies):
        wait_send(cs)


def gauss():
    taps = np.arange(-GAUSS_RADIUS, GAUSS_RADIUS + 1)
    w = np.exp(-(taps * taps) / (2.0 * GAUSS_SIGMA**2))
    return w / w.sum()


def as_pair(m):
    h = m.astype(jnp.bfloat16)
    return h, (m - h.astype(np.float64)).astype(jnp.bfloat16)


def gauss_y(cols):
    w, wide = gauss(), cols + BY
    m = np.zeros((wide, cols))
    for j in range(cols):
        for t in range(-GAUSS_RADIUS, GAUSS_RADIUS + 1):
            m[(j + t) % wide, j] = w[t + GAUSS_RADIUS]
    return as_pair(m)


def gauss_zx(depth, rows):
    w = gauss()
    mx = np.zeros((rows, rows + 2 * GHALO))
    mz = np.zeros((depth, depth))
    for t in range(-GAUSS_RADIUS, GAUSS_RADIUS + 1):
        for r in range(rows):
            mx[r, r + GHALO + t] = w[t + GAUSS_RADIUS]
        for z in range(depth):
            if 0 <= z + t < depth:
                mz[z, z + t] = w[t + GAUSS_RADIUS]
    return as_pair(-STEP_RATE * np.kron(mz, mx))


def on_device(nx, ny, moving, fixed, velocity, offsets, tissue):
    depth, rows, cols = moving.shape
    ext, wide, gext = rows + 2 * HALO, cols + BY, rows + 2 * GHALO

    def ring(n):
        packs = -(-n // PACK)
        return (
            pltpu.VMEM((n, ext, wide), BF16),
            pltpu.VMEM((packs, rows, BY), BF16),
            pltpu.VMEM((packs, rows, BY), BF16),
            pltpu.VMEM((packs, ext, BY), BF16),
            pltpu.VMEM((packs, ext, BY), BF16),
        )

    vmem = pl.BlockSpec(memory_space=pltpu.VMEM)
    smem = pl.BlockSpec(memory_space=pltpu.SMEM)
    gshape = (3, depth, gext, wide)
    hbm = pl.BlockSpec(memory_space=pl.ANY)
    consts = gauss_y(cols) + gauss_zx(depth, rows)
    update, loss = pl.pallas_call(
        functools.partial(fused_kernel, nx, ny),
        out_shape=(
            jax.ShapeDtypeStruct((3, depth, rows, cols), F32),
            jax.ShapeDtypeStruct((1, 1), F32),
        ),
        in_specs=[smem, smem, vmem, vmem, hbm, hbm, hbm, hbm, hbm],
        out_specs=(hbm, vmem),
        scratch_shapes=[
            ring(depth), ring(depth + 1), ring(depth), ring(3 * depth),
            pltpu.VMEM(velocity.shape, F32),
            pltpu.VMEM((3, depth, rows, cols), F32),
            pltpu.VMEM((depth + 2 * (ZREACH + 1), 2 * BX, 2 * BY), F32),
            pltpu.VMEM((5, depth + 2 * BOX, ext, wide), F32),
            pltpu.VMEM((3, depth + 2 * BOX, ext, wide), F32),
            pltpu.VMEM((wide, wide), BF16),
            pltpu.VMEM(gshape, BF16),
            pltpu.VMEM(gshape, BF16),
            pltpu.VMEM((3, depth, rows, cols), F32),
            *[pltpu.VMEM(c.shape, BF16) for c in consts],
            pltpu.VMEM((ext, wide), F32),
            pltpu.VMEM((ext, wide), F32),
            pltpu.VMEM((ext, wide), F32),
            pltpu.VMEM((2, 16, BY), F32),
            pltpu.VMEM((ny, 16, BY), F32),
            pltpu.VMEM((nx, 16, BY), F32),
            pltpu.SemaphoreType.DMA,
            pltpu.SemaphoreType.DMA((4,)),
            pltpu.SemaphoreType.DMA((3,)),
            pltpu.SemaphoreType.DMA((4, 8)),
            pltpu.SemaphoreType.DMA((4, 8)),
            pltpu.SemaphoreType.DMA((ny,)),
            pltpu.SemaphoreType.DMA((ny,)),
            pltpu.SemaphoreType.DMA((nx,)),
            pltpu.SemaphoreType.DMA((nx,)),
        ],
        compiler_params=pltpu.CompilerParams(
            collective_id=0, has_side_effects=True, vmem_limit_bytes=56 * 2**20
        ),
    )(offsets, tissue, moving, fixed, velocity, *[jnp.asarray(c) for c in consts])
    return update, loss[0, 0]


def solution(mesh):
    in_specs = (
        P(None, "gx", "gy"),
        P(None, "gx", "gy"),
        P(None, None, "gx", "gy"),
        P(None, "gx", "gy"),
        P("gx", "gy"),
    )
    out_specs = (P(None, None, "gx", "gy"), P())
    return jax.shard_map(
        functools.partial(on_device, mesh.shape["gx"], mesh.shape["gy"]),
        mesh=mesh, in_specs=in_specs, out_specs=out_specs, check_vma=False,
    )
```

```python
import functools
import math

import jax
import jax.numpy as jnp
from jax import lax
from jax.experimental import pallas as pl
from jax.experimental.pallas import tpu as pltpu
from jax.sharding import PartitionSpec as P

BX = 16
BY = 128
ZREACH = 2
BOX = 4
GAUSS_RADIUS = 7
GAUSS_SIGMA = 3.0
COUNT = 729.0
EPS = 1e-05
STEP_RATE = 16.0
HALO = 16
GHALO = 8
PACK = BY // HALO
GROUP = 4
F32 = jnp.float32
BF16 = jnp.bfloat16
MESH = pl.DeviceIdType.MESH

DIRS = [(-1, 0), (1, 0), (0, -1), (0, 1), (-1, -1), (-1, 1), (1, -1), (1, 1)]


def dot(a, b):
    return jnp.dot(a, b, preferred_element_type=F32)


def split2(x):
    h = x.astype(BF16)
    return h, (x - h.astype(F32)).astype(BF16)


def split3(x):
    h = x.astype(BF16)
    r = x - h.astype(F32)
    m = r.astype(BF16)
    return h, m, (r - m.astype(F32)).astype(BF16)


def halo_refs(direction, rows, center, to_left, to_right, left, right, *thin):
    dx, dy = direction
    cols = center.shape[2] - BY
    dst_rows = {-1: pl.ds(HALO + rows, HALO), 0: pl.ds(HALO, rows), 1: pl.ds(0, HALO)}[dx]
    if dy == 0 and thin:
        up, down, top, bottom = thin
        return (up, bottom) if dx < 0 else (down, top)
    if dy == 0:
        src_rows = pl.ds(HALO, HALO) if dx < 0 else pl.ds(rows, HALO)
        own = pl.ds(0, cols)
        return center.at[:, src_rows, own], center.at[:, dst_rows, own]
    src_rows = {-1: pl.ds(0, HALO), 0: pl.ds(0, rows), 1: pl.ds(rows - HALO, HALO)}[dx]
    if dy < 0:
        return to_left.at[:, src_rows, :], right.at[:, dst_rows, :]
    return to_right.at[:, src_rows, :], left.at[:, dst_rows, :]


def groups_of(planes, body):
    def step(g, carry):
        body(g * PACK, g, PACK)
        return carry

    lax.fori_loop(0, planes // PACK, step, 0)
    if planes % PACK:
        body(planes - planes % PACK, planes // PACK, planes % PACK)


def turn(x, shift, axis):
    shift %= x.shape[axis]
    return x if shift == 0 else pltpu.roll(x, shift, axis)


def pack(center, to_left, to_right, rows):
    cols = center.shape[2] - BY
    lane = lax.broadcasted_iota(jnp.int32, (rows, BY), 1)

    def body(z, g, count):
        l = jnp.zeros((rows, BY), F32)
        r = jnp.zeros((rows, BY), F32)
        for i in range(count):
            mine = jnp.logical_and(lane >= i * HALO, lane < (i + 1) * HALO)
            a = center[z + i, HALO : HALO + rows, 0:BY].astype(F32)
            b = center[z + i, HALO : HALO + rows, cols - BY : cols].astype(F32)
            l = jnp.where(mine, turn(a, i * HALO, 1), l)
            r = jnp.where(mine, turn(b, (i + 1) * HALO, 1), r)
        to_left[g] = l.astype(BF16)
        to_right[g] = r.astype(BF16)

    groups_of(center.shape[0], body)


def pack_rows(center, up, down, rows):
    cols = center.shape[2] - BY

    def body(g, carry):
        for i in range(4):
            h = g * 4 + i
            a = center[2 * h, HALO : HALO + rows, 0:cols].astype(F32)
            b = center[2 * h + 1, HALO : HALO + rows, 0:cols].astype(F32)
            up[h] = jnp.concatenate([a[:GHALO], b[:GHALO]], axis=0).astype(BF16)
            down[h] = jnp.concatenate([a[-GHALO:], b[-GHALO:]], axis=0).astype(BF16)
        return carry

    lax.fori_loop(0, center.shape[0] // 8, body, 0)


def unpack_rows(center, top, bottom, rows):
    cols = center.shape[2] - BY
    none = jnp.zeros((HALO - GHALO, cols), F32)

    def body(g, carry):
        for i in range(4):
            h = g * 4 + i
            t, b = top[h].astype(F32), bottom[h].astype(F32)
            for j in range(2):
                part = slice(j * GHALO, (j + 1) * GHALO)
                center[2 * h + j, 0:HALO, 0:cols] = jnp.concatenate(
                    [none, t[part]], axis=0
                ).astype(BF16)
                center[2 * h + j, HALO + rows : 2 * HALO + rows, 0:cols] = jnp.concatenate(
                    [b[part], none], axis=0
                ).astype(BF16)
        return carry

    lax.fori_loop(0, center.shape[0] // 8, body, 0)


def unpack(center, left, right):
    _, ext, wide = center.shape
    lane = lax.broadcasted_iota(jnp.int32, (ext, BY), 1)

    def body(z, g, count):
        l, r = left[g].astype(F32), right[g].astype(F32)
        for i in range(count):
            v = jnp.where(lane < HALO, turn(r, -i * HALO, 1), 0.0)
            v = jnp.where(lane >= BY - HALO, turn(l, -(i + 1) * HALO, 1), v)
            center[z + i, :, wide - BY : wide] = v.astype(BF16)

    groups_of(center.shape[0], body)


def window_x(v):
    s = v + turn(v, 1, 0) + turn(v, -1, 0)
    return s + turn(s, 3, 0) + turn(s, -3, 0)


def fused_kernel(
    nx, ny,
    off_ref, tis_ref, mov_ref, fix_ref, vel_hbm,
    out_hbm, loss_ref,
    m, f, w, s,
    vel, sF, T, Y, A, by_ref,
    gh_ref, gl_ref, out, yh, yl, xh, xl, acc_ref, mask_ref, own_ref, part, by_y, by_x,
    vel_sem, out_sem, send_sem, recv_sem, ysend_sem, yrecv_sem, xsend_sem, xrecv_sem,
):
    (mC, fC, wC, sC) = (m[0], f[0], w[0], s[0])
    depth, rows, cols = mov_ref.shape
    ext = rows + 2 * HALO
    wide = cols + BY
    gx, gy = lax.axis_index("gx"), lax.axis_index("gy")

    def exists(d):
        dx, dy = d
        c = None
        for cond in (
            (gx > 0) if dx < 0 else (gx < nx - 1) if dx > 0 else None,
            (gy > 0) if dy < 0 else (gy < ny - 1) if dy > 0 else None,
        ):
            if cond is not None:
                c = cond if c is None else jnp.logical_and(c, cond)
        return c

    has = [exists(d) for d in DIRS]

    vel_copy = pltpu.make_async_copy(vel_hbm, vel, vel_sem)
    vel_copy.start()
    barrier = pltpu.get_barrier_semaphore()
    for i, (dx, dy) in enumerate(DIRS):
        @pl.when(has[i])
        def _():
            pl.semaphore_signal(barrier, inc=1, device_id=(gx + dx, gy + dy), device_id_type=MESH)

    for d in range(1, ny):
        pl.semaphore_signal(
            barrier, inc=1, device_id=(gx, lax.rem(gy + d, ny)), device_id_type=MESH
        )
    for d in range(1, nx):
        pl.semaphore_signal(
            barrier, inc=1, device_id=(lax.rem(gx + d, nx), gy), device_id_type=MESH
        )

    def clear(*bufs):
        for i, (dx, dy) in enumerate(DIRS):
            _, dst = halo_refs((-dx, -dy), rows, *bufs)

            @pl.when(jnp.logical_not(has[i]))
            def _():
                dst[...] = jnp.zeros(dst.shape, dst.dtype)

    mC[:, HALO : HALO + rows, 0:cols] = mov_ref[...]
    pack_rows(m[0], m[5], m[6], rows)
    pack(m[0], m[1], m[2], rows)
    def line(g, n):
        return 1 + jnp.where(g > 0, 1, 0) + jnp.where(g < n - 1, 1, 0)

    pl.semaphore_wait(barrier, line(gx, nx) * line(gy, ny) - 1 + (ny - 1) + (nx - 1))

    def copies(t, *bufs):
        out = []
        for i, (dx, dy) in enumerate(DIRS):
            src, dst = halo_refs((dx, dy), rows, *bufs)
            out.append(
                pltpu.make_async_remote_copy(
                    src_ref=src, dst_ref=dst,
                    send_sem=send_sem.at[t, i], recv_sem=recv_sem.at[t, i],
                    device_id=(gx + dx, gy + dy), device_id_type=MESH,
                )
            )
        return out

    def start(cs):
        for i, c in enumerate(cs):
            @pl.when(has[i])
            def _():
                c.start()

    def wait_recv(cs):
        for i, c in enumerate(cs):
            j = DIRS.index((-DIRS[i][0], -DIRS[i][1]))

            @pl.when(has[j])
            def _():
                c.wait_recv()

    def wait_send(cs):
        for i, c in enumerate(cs):
            @pl.when(has[i])
            def _():
                c.wait_send()

    m_copies = copies(0, *m)
    f_copies = copies(1, *f)
    w_copies = copies(2, *w)
    s_copies = copies(3, *s)
    start(m_copies)

    fC[0:depth, HALO : HALO + rows, 0:cols] = fix_ref[...]
    for r in range(rows // BX):
        for c in range(cols // BY):
            value = tis_ref[r, c].astype(F32)
            fC[depth, HALO + r * BX : HALO + (r + 1) * BX, c * BY : (c + 1) * BY] = jnp.full(
                (BX, BY), value, F32
            ).astype(BF16)
    pack(f[0], f[1], f[2], rows)
    start(f_copies)

    clear(*m)
    clear(*f)
    clear(*w)
    clear(*s)

    ki = lax.broadcasted_iota(jnp.int32, (wide, wide), 0)
    ji = lax.broadcasted_iota(jnp.int32, (wide, wide), 1)
    dist = jnp.abs(ki - ji)
    dist = jnp.minimum(dist, wide - dist)
    by_ref[...] = jnp.where(dist <= BOX, 1.0, 0.0).astype(BF16)
    yh[...], yl[...] = gauss_y(wide, cols)
    zpad = ZREACH + 1
    T[0:zpad] = jnp.zeros((zpad,) + T.shape[1:], F32)
    T[depth + zpad :] = jnp.zeros((zpad,) + T.shape[1:], F32)
    for k in range(5):
        Y[k, 0:BOX] = jnp.zeros((BOX, ext, wide), F32)
        Y[k, depth + BOX :] = jnp.zeros((BOX, ext, wide), F32)
    for k in range(3):
        A[k, 0:BOX] = jnp.zeros((BOX, ext, wide), F32)
        A[k, depth + BOX :] = jnp.zeros((BOX, ext, wide), F32)

    wait_recv(m_copies)
    unpack_rows(m[0], m[7], m[8], rows)
    unpack(m[0], m[3], m[4])
    vel_copy.wait()

    slab = BX + 2 * HALO
    for br in range(rows // BX):
        for bc in range(cols // BY):
            oz, ox, oy = off_ref[0, br, bc], off_ref[1, br, bc], off_ref[2, br, bc]
            lane = lax.broadcasted_iota(jnp.int32, (wide, 2 * BY), 1)
            target = jnp.where(lane < BY, lane, lane - BY + 1) + bc * BY + oy
            target = jnp.where(target < 0, target + wide, target)
            source = lax.broadcasted_iota(jnp.int32, (wide, 2 * BY), 0)
            shift = jnp.where(source == target, 1.0, 0.0).astype(BF16)
            r0 = br * BX
            i = lax.broadcasted_iota(jnp.int32, (GROUP * 2 * BX, GROUP * slab), 0)
            k = lax.broadcasted_iota(jnp.int32, (GROUP * 2 * BX, GROUP * slab), 1)
            row = (i // (2 * BX)) * slab + HALO + (i % BX) + (i // BX) % 2 + ox
            down = jnp.where(k == row, 1.0, 0.0).astype(BF16)

            def move(g, carry):
                z = pl.multiple_of(g * GROUP, GROUP)
                x = mC[pl.ds(z, GROUP), r0 : r0 + slab, :]
                t = dot(x.reshape(GROUP * slab, wide), shift).astype(BF16)
                T[pl.ds(z + zpad, GROUP)] = dot(down, t).reshape(GROUP, 2 * BX, 2 * BY)
                return carry

            lax.fori_loop(0, depth // GROUP, move, 0)
            rs = slice(r0, r0 + BX)
            cs = slice(bc * BY, (bc + 1) * BY)
            hs = slice(HALO + r0, HALO + r0 + BX)

            def warp(z, carry):
                f0, f1, f2 = vel[0, z, rs, cs], vel[1, z, rs, cs], vel[2, z, rs, cs]
                planes, slopes_x, slopes_y = [], [], []
                for c in (0, 1):
                    vs, ds = [], []
                    for a in (0, 1):
                        s = T[z + zpad + oz + c, a * BX : (a + 1) * BX, :]
                        low, high = s[:, :BY], s[:, BY:]
                        d = high - low
                        vs.append((1.0 - f2) * low + f2 * high)
                        ds.append(d)
                    planes.append((1.0 - f1) * vs[0] + f1 * vs[1])
                    slopes_x.append(vs[1] - vs[0])
                    slopes_y.append((1.0 - f1) * ds[0] + f1 * ds[1])
                value = (1.0 - f0) * planes[0] + f0 * planes[1]
                wC[z, hs, cs] = value.astype(BF16)
                slopes = (
                    planes[1] - planes[0],
                    (1.0 - f0) * slopes_x[0] + f0 * slopes_x[1],
                    (1.0 - f0) * slopes_y[0] + f0 * slopes_y[1],
                )
                for k in range(3):
                    sF[k, z, rs, cs] = slopes[k]
                    sC[k * depth + z, hs, cs] = slopes[k].astype(BF16)
                return carry

            def warp_group(g, carry):
                for t in range(GROUP):
                    warp(g * GROUP + t, carry)
                return carry

            lax.fori_loop(0, depth // GROUP, warp_group, 0)

    pack(w[0], w[1], w[2], rows)
    start(w_copies)
    pack_rows(s[0], s[5], s[6], rows)
    pack(s[0], s[1], s[2], rows)
    start(s_copies)
    wait_recv(f_copies)
    unpack(f[0], f[3], f[4])

    by = by_ref[...]

    def fixed_y(g, carry):
        z = g * GROUP
        j_low = fC[pl.ds(z, GROUP)].reshape(GROUP * ext, wide)
        j = j_low.astype(F32)
        h, l = split2(j * j)
        Y[1, pl.ds(z + BOX, GROUP)] = dot(j_low, by).reshape(GROUP, ext, wide)
        Y[3, pl.ds(z + BOX, GROUP)] = (dot(h, by) + dot(l, by)).reshape(GROUP, ext, wide)
        return carry

    lax.fori_loop(0, depth // GROUP, fixed_y, 0)
    for z in range(depth):
        xh[z * rows : (z + 1) * rows], xl[z * rows : (z + 1) * rows] = gauss_zx(rows, depth, z)
    wait_recv(w_copies)
    unpack(w[0], w[3], w[4])

    def stats_y(g, carry):
        z = g * GROUP
        i_low = wC[pl.ds(z, GROUP)].reshape(GROUP * ext, wide)
        i = i_low.astype(F32)
        j = fC[pl.ds(z, GROUP)].reshape(GROUP * ext, wide).astype(F32)
        fields = [(0, (i_low,)), (2, split2(i * i)), (4, split2(i * j))]
        for k, parts in fields:
            y = dot(parts[0], by)
            for part in parts[1:]:
                y = y + dot(part, by)
            Y[k, pl.ds(z + BOX, GROUP)] = y.reshape(GROUP, ext, wide)
        return carry

    lax.fori_loop(0, depth // GROUP, stats_y, 0)

    def window_z(ref, k, z, tile):
        p = [ref[k, z + t, :, tile] for t in range(GROUP + 2 * BOX)]
        common = ((p[3] + p[4]) + (p[5] + p[6])) + (p[7] + p[8])
        low, high = p[1] + p[2], p[9] + p[10]
        outs = [
            common + (p[0] + low), common + (low + p[9]),
            common + (p[2] + high), common + (high + p[11]),
        ]
        return window_x(jnp.concatenate(outs, axis=0))

    tiles = [slice(c, c + BY) for c in range(0, wide, BY)]

    row = lax.broadcasted_iota(jnp.int32, (ext, wide), 0)
    lane = lax.broadcasted_iota(jnp.int32, (ext, wide), 1)
    own_row = jnp.logical_and(row >= HALO, row < HALO + rows)
    acc_ref[...] = jnp.zeros_like(acc_ref)
    reach = HALO - BOX - 1
    near = jnp.logical_and(row >= HALO - reach, row < HALO + rows + reach)
    near = jnp.logical_and(near, jnp.logical_or(lane < cols + reach, lane >= wide - reach))
    mask_ref[...] = jnp.where(near, fC[depth].astype(F32), 0.0)
    own_ref[...] = jnp.where(jnp.logical_and(own_row, lane < cols), mask_ref[...], 0.0)

    def stats(g, carry):
        z = g * GROUP
        terms = [[], [], []]
        for tile in tiles:
            si, sj, sii, sjj, sij = [
                window_z(Y, k, z, tile).reshape(GROUP, ext, BY) for k in range(5)
            ]
            cross = sij - si * sj * (1.0 / COUNT)
            var_i = sii - si * si * (1.0 / COUNT)
            var_j = sjj - sj * sj * (1.0 / COUNT)
            q = cross / (var_i * var_j + EPS)
            live = mask_ref[:, tile][None] > 0.0
            if tile.start < cols:
                own = own_ref[:, tile][None] > 0.0
                acc_ref[:, tile] += jnp.sum(jnp.where(own, cross * q, 0.0), axis=0)
            q = jnp.where(live, q, 0.0)
            p = q * q * var_j
            values = ((2.0 / COUNT) * (q * sj - p * si), p, -2.0 * q)
            for k in range(3):
                terms[k].append(values[k].reshape(GROUP * ext, BY).astype(BF16))
        for k in range(3):
            y = dot(jnp.concatenate(terms[k], axis=1), by_ref[...])
            A[k, pl.ds(z + BOX, GROUP)] = y.reshape(GROUP, ext, wide)
        return carry

    lax.fori_loop(0, depth // GROUP, stats, 0)

    def folded(x):
        x = sum(x[r : r + 8] for r in range(0, ext, 8))
        return sum(x[:, c : c + BY] for c in range(0, wide, BY))

    blocks = 0
    for r in range(rows // BX):
        for c in range(cols // BY):
            blocks = blocks + tis_ref[r, c]
    part[0, 0:8] = folded(acc_ref[...])
    part[0, 8:16] = jnp.full((8, BY), blocks.astype(F32), F32)

    def spread(n, axis_of, src, dst, ssem, rsem):
        return [
            pltpu.make_async_remote_copy(
                src_ref=src, dst_ref=dst.at[d], send_sem=ssem.at[d], recv_sem=rsem.at[d],
                device_id=axis_of(d), device_id_type=MESH,
            )
            for d in range(1, n)
        ]

    y_copies = spread(
        ny, lambda d: (gx, lax.rem(gy + d, ny)), part.at[0], by_y, ysend_sem, yrecv_sem
    )
    x_copies = spread(
        nx, lambda d: (lax.rem(gx + d, nx), gy), part.at[1], by_x, xsend_sem, xrecv_sem
    )
    for c in y_copies:
        c.start()

    wait_recv(s_copies)
    unpack_rows(s[0], s[7], s[8], rows)
    unpack(s[0], s[3], s[4])
    inner = slice(HALO - GHALO, HALO + rows + GHALO)

    def grads(g, carry):
        z = g * GROUP
        for tile in tiles:
            box = [
                window_z(A, k, z, tile).reshape(GROUP, ext, BY)[:, inner] for k in range(3)
            ]
            i = wC[pl.ds(z, GROUP), :, tile].astype(F32)[:, inner]
            j = fC[pl.ds(z, GROUP), :, tile].astype(F32)[:, inner]
            grad = box[0] + 2.0 * i * box[1] + j * box[2]
            for k in range(3):
                c = sC[pl.ds(k * depth + z, GROUP), :, tile].astype(F32)
                if tile.start < cols:
                    c = jnp.concatenate(
                        [c[:, HALO - GHALO : HALO], sF[k, pl.ds(z, GROUP), :, tile],
                         c[:, HALO + rows : HALO + rows + GHALO]], axis=1)
                else:
                    c = c[:, inner]
                h, l = split2(grad * c)
                gh_ref[k, pl.ds(z, GROUP), :, tile] = h
                gl_ref[k, pl.ds(z, GROUP), :, tile] = l
        return carry

    lax.fori_loop(0, depth // GROUP, grads, 0)

    for c in y_copies:
        c.wait()
    total = part[0]
    for d in range(1, ny):
        total = total + by_y[d]
    part[1] = total
    for c in x_copies:
        c.start()

    out_copies = []
    for k in range(3):
        h = gh_ref[k].reshape(depth * (rows + 2 * GHALO), wide)
        l = gl_ref[k].reshape(depth * (rows + 2 * GHALO), wide)
        t = dot(h, yh[...]) + dot(l, yh[...]) + dot(h, yl[...])
        h, l = split2(t)
        o = dot(xh[...], h) + dot(xh[...], l) + dot(xl[...], h)
        out[k] = o.reshape(depth, rows, cols)
        copy = pltpu.make_async_copy(out.at[k], out_hbm.at[k], out_sem.at[k])
        copy.start()
        out_copies.append(copy)

    for c in x_copies:
        c.wait()
    total = part[1]
    for d in range(1, nx):
        total = total + by_x[d]
    tissue_total = jnp.max(total[8:16], keepdims=True)
    loss_ref[...] = -jnp.sum(total[0:8], keepdims=True) / (
        tissue_total * float(BX * BY * depth)
    )
    for c in out_copies:
        c.wait()
    for cs in (m_copies, f_copies, w_copies, s_copies):
        wait_send(cs)


def gauss_scale():
    taps = range(-GAUSS_RADIUS, GAUSS_RADIUS + 1)
    return 1.0 / sum(math.exp(-float(t * t) / (2.0 * GAUSS_SIGMA**2)) for t in taps)


def gauss_y(wide, cols):
    k = lax.broadcasted_iota(jnp.int32, (wide, cols), 0)
    j = lax.broadcasted_iota(jnp.int32, (wide, cols), 1)
    d = jnp.abs(k - j)
    d = jnp.minimum(d, wide - d)
    t = d.astype(F32)
    e = jnp.exp(t * t * (-0.5 / GAUSS_SIGMA**2)) * gauss_scale()
    return split2(jnp.where(d <= GAUSS_RADIUS, e, 0.0))


def gauss_zx(rows, depth, z):
    gext = rows + 2 * GHALO
    k = lax.broadcasted_iota(jnp.int32, (1, depth * gext), 1).astype(F32)
    kz = jnp.floor((k + 0.5) * (1.0 / gext))
    kx = k - kz * gext - GHALO
    r = lax.broadcasted_iota(jnp.int32, (rows, 1), 0).astype(F32)
    dz, dx = jnp.abs(kz - z), jnp.abs(kx - r)
    far = jnp.where(dz > GAUSS_RADIUS, 1e4, dz * dz) + jnp.where(
        dx > GAUSS_RADIUS, 1e4, dx * dx
    )
    e = jnp.exp(far * (-0.5 / GAUSS_SIGMA**2)) * (-STEP_RATE * gauss_scale() ** 2)
    return split2(e)


def on_device(nx, ny, moving, fixed, velocity, offsets, tissue):
    depth, rows, cols = moving.shape
    ext, wide, gext = rows + 2 * HALO, cols + BY, rows + 2 * GHALO

    def ring(n, thin=False):
        packs = -(-n // PACK)
        return (
            pltpu.VMEM((n, ext, wide), BF16),
            pltpu.VMEM((packs, rows, BY), BF16),
            pltpu.VMEM((packs, rows, BY), BF16),
            pltpu.VMEM((packs, ext, BY), BF16),
            pltpu.VMEM((packs, ext, BY), BF16),
            *[pltpu.VMEM((n // 2, 2 * GHALO, cols), BF16)] * (4 if thin else 0),
        )

    vmem = pl.BlockSpec(memory_space=pltpu.VMEM)
    smem = pl.BlockSpec(memory_space=pltpu.SMEM)
    gshape = (3, depth, gext, wide)
    hbm = pl.BlockSpec(memory_space=pl.ANY)
    update, loss = pl.pallas_call(
        functools.partial(fused_kernel, nx, ny),
        out_shape=(
            jax.ShapeDtypeStruct((3, depth, rows, cols), F32),
            jax.ShapeDtypeStruct((1, 1), F32),
        ),
        in_specs=[smem, smem, vmem, vmem, hbm],
        out_specs=(hbm, vmem),
        scratch_shapes=[
            ring(depth, True), ring(depth + 1), ring(depth), ring(3 * depth, True),
            pltpu.VMEM(velocity.shape, F32),
            pltpu.VMEM((3, depth, rows, cols), F32),
            pltpu.VMEM((depth + 2 * (ZREACH + 1), 2 * BX, 2 * BY), F32),
            pltpu.VMEM((5, depth + 2 * BOX, ext, wide), F32),
            pltpu.VMEM((3, depth + 2 * BOX, ext, wide), F32),
            pltpu.VMEM((wide, wide), BF16),
            pltpu.VMEM(gshape, BF16),
            pltpu.VMEM(gshape, BF16),
            pltpu.VMEM((3, depth, rows, cols), F32),
            *[pltpu.VMEM((wide, cols), BF16)] * 2,
            *[pltpu.VMEM((depth * rows, depth * gext), BF16)] * 2,
            pltpu.VMEM((ext, wide), F32),
            pltpu.VMEM((ext, wide), F32),
            pltpu.VMEM((ext, wide), F32),
            pltpu.VMEM((2, 16, BY), F32),
            pltpu.VMEM((ny, 16, BY), F32),
            pltpu.VMEM((nx, 16, BY), F32),
            pltpu.SemaphoreType.DMA,
            pltpu.SemaphoreType.DMA((3,)),
            pltpu.SemaphoreType.DMA((4, 8)),
            pltpu.SemaphoreType.DMA((4, 8)),
            pltpu.SemaphoreType.DMA((ny,)),
            pltpu.SemaphoreType.DMA((ny,)),
            pltpu.SemaphoreType.DMA((nx,)),
            pltpu.SemaphoreType.DMA((nx,)),
        ],
        compiler_params=pltpu.CompilerParams(
            collective_id=0, has_side_effects=True, vmem_limit_bytes=48 * 2**20
        ),
    )(offsets, tissue, moving, fixed, velocity)
    return update, loss[0, 0]


def solution(mesh):
    in_specs = (
        P(None, "gx", "gy"),
        P(None, "gx", "gy"),
        P(None, None, "gx", "gy"),
        P(None, "gx", "gy"),
        P("gx", "gy"),
    )
    out_specs = (P(None, None, "gx", "gy"), P())
    return jax.shard_map(
        functools.partial(on_device, mesh.shape["gx"], mesh.shape["gy"]),
        mesh=mesh, in_specs=in_specs, out_specs=out_specs, check_vma=False,
    )
```
